32 devices in a mesh: ingest: 16 (over z, y, x), span: 2 (over core).
Axes of the slice: x: 2, y: 2, z: 4, core: 2. Of those that a mesh axis runs over, the one named last changes fastest.
Arguments:
- embeddings: bfloat16 [16384, 768], P(('ingest', 'span')), may hold values from -100 to 100
- cluster_id: int32 [16384], P(('ingest', 'span')), may hold values from 0 to 15, as said below
- rank: int32 [16384], P(('ingest', 'span')), may hold values from 0 to 16383, each once
Outputs:
- max_cosine: float32 [16384], P(('ingest', 'span'))
The draws below stay inside these ranges and needn't reach their ends.
Inputs may be any that keep to these rules, and one draw needn't show every extreme that they name: `cluster_id`: the 512 embeddings of each device name one cluster at most 64 times, and some cluster exactly 64 times. `rank`: every value once.
All inputs are finite; a program needn't handle non-finite values.
Results may differ from the reference program's by a relative error of at most 0.00054.
Values may be sent and summed in bfloat16 or wider, within the bound.
No kernel may reach another device: no remote copies, remote signals or barrier semaphores. Data moves between devices by JAX's collectives and lax.ppermute only.
A program may use at most 64 MiB of HBM per device.

```python
import math
import jax
import jax.numpy as jnp
from jax import lax

D = 768
ROWS_DEV = 512
CAP = 64
NCLUST = 16
ROWS = 16384
DEVICES = 32


def assign_clusters(key):
    blocks = ROWS // ROWS_DEV
    first_key, second_key, third_key = jax.random.split(key, 3)
    heaviness = jax.random.randint(first_key, (NCLUST,), 0, 4)
    jitter = jax.random.randint(second_key, (blocks, NCLUST), 0, 65536)
    scores = (heaviness[None, :] * 65536 + jitter) * NCLUST + jnp.arange(NCLUST, dtype=jnp.int32)[None, :]
    ordering = jnp.argsort(-scores, axis=1).astype(jnp.int32)
    positions = jnp.arange(ROWS_DEV, dtype=jnp.int32)
    half_rows = ROWS_DEV // 2
    quarter = NCLUST // 4
    groups = jnp.where(positions < half_rows, positions // CAP, quarter + (positions - half_rows) % (NCLUST - quarter))
    shuffles = jax.vmap(lambda sub_key: jax.random.permutation(sub_key, ROWS_DEV))(jax.random.split(third_key, blocks))
    shuffled = groups[shuffles]
    chosen = jnp.take_along_axis(ordering, shuffled, axis=1)
    return chosen.reshape(ROWS).astype(jnp.int32)


def draw_cluster_id(key, part):
    clusters = assign_clusters(key)
    return clusters


def draw_embeddings(key, part):
    clusters = assign_clusters(key)
    key = jax.random.fold_in(key, 7)
    streams = jax.random.split(key, 5)
    centers = jax.random.normal(streams[0], (NCLUST, D), jnp.float32)
    noise = jax.random.normal(streams[1], (ROWS, D), jnp.float32)
    mixing = jnp.exp(jax.random.uniform(streams[2], (ROWS, 1), jnp.float32, math.log(0.3), math.log(3.0)))
    scaling = jnp.exp(jax.random.uniform(streams[3], (ROWS, 1), jnp.float32, math.log(0.5), math.log(5.0)))
    columns = jnp.exp(jax.random.uniform(streams[4], (1, D), jnp.float32, -0.7, 0.7))
    values = scaling * (mixing * centers[clusters] + noise) * columns
    return jnp.clip(values, -100.0, 100.0).astype(jnp.bfloat16)


def setup_inputs(seed: int = 0) -> dict:
    key_of = jax.random.split(jax.random.key(seed), 4)
    return {
        "embeddings": draw_embeddings(jax.random.fold_in(key_of[3], 71), 0),
        "cluster_id": draw_cluster_id(jax.random.fold_in(key_of[3], 71), 0),
        "rank": jax.random.permutation(key_of[2], ROWS).astype(jnp.int32),
    }


def normalize(embeddings):
    widened = embeddings.astype(jnp.float32)
    return (widened * lax.rsqrt(lax.optimization_barrier(jnp.sum(widened * widened, axis=1, keepdims=True)) + 1e-06)).astype(jnp.bfloat16)

def reference(embeddings, cluster_id, rank):
    normed = normalize(embeddings)
    window = DEVICES * CAP
    ordering = jnp.argsort(cluster_id, stable=True).astype(jnp.int32)
    sorted_ids = cluster_id[ordering]
    sorted_units = normed[ordering].astype(jnp.float32)
    sorted_rank = rank[ordering]
    starts = jnp.searchsorted(sorted_ids, jnp.arange(NCLUST, dtype=jnp.int32)).astype(jnp.int32)
    padded_units = jnp.concatenate([sorted_units, jnp.zeros((window, D), jnp.float32)], axis=0)
    padded_ids = jnp.concatenate([sorted_ids, jnp.full((window,), -1, jnp.int32)], axis=0)
    padded_rank = jnp.concatenate([sorted_rank, jnp.zeros((window,), jnp.int32)], axis=0)

    def visit_cluster(result, cluster):
        offset = starts[cluster]
        window_rows = lax.dynamic_slice_in_dim(padded_units, offset, window, 0)
        window_ids = lax.dynamic_slice_in_dim(padded_ids, offset, window, 0)
        window_rank = lax.dynamic_slice_in_dim(padded_rank, offset, window, 0)
        members = window_ids == cluster
        scores = jnp.dot(window_rows, window_rows.T, precision=lax.Precision.HIGHEST)
        earlier = members[None, :] & (window_rank[None, :] < window_rank[:, None])
        highest = lax.optimization_barrier(jnp.max(jnp.where(earlier, scores, -1.0), axis=1))
        previous = lax.dynamic_slice_in_dim(result, offset, window, 0)
        result = lax.dynamic_update_slice_in_dim(result, jnp.where(members, highest, previous).astype(result.dtype), offset, 0)
        return (result, None)
    result, _ = lax.scan(visit_cluster, jnp.full((ROWS + window,), -1.0, jnp.float32), jnp.arange(NCLUST, dtype=jnp.int32))
    return jnp.zeros((ROWS,), jnp.float32).at[ordering].set(result[:ROWS])
```

```python
import functools

import jax
import jax.numpy as jnp
from jax import lax
from jax.experimental import pallas as pl
from jax.experimental.pallas import tpu as pltpu
from jax.sharding import PartitionSpec as P

LANES = 128
EXTRA = 8
NEVER = 2.0**24
TILE = 512
PARAMS = pltpu.CompilerParams(vmem_limit_bytes=40 * 2**20)
VMEM = pl.BlockSpec(memory_space=pltpu.VMEM)
SMEM = pl.BlockSpec(memory_space=pltpu.SMEM)
ANY = pl.BlockSpec(memory_space=pl.ANY)


LIGHT = pl.CostEstimate(flops=1, bytes_accessed=1, transcendentals=0)


def membership(cid, nodes, rows):
    return lax.broadcasted_iota(jnp.int32, (nodes, rows), 0) == cid


def partners(nodes):
    half = nodes // 2
    far = [half, nodes - 1, *range(half + half // 2, nodes - 1), *range(half + 1, half + half // 2)]
    near = [1, *range(half // 2, half), *range(2, half // 2)]
    sequence = [far[0]]
    for pair in zip(near, far[1:]):
        sequence.extend(pair)
    flips = [0] * nodes
    for g, flip in zip([*range(half + 3, nodes), *range(half, half + 3), *range(1, half)], sequence):
        flips[g] = flip
    return flips


def place_kernel(me_ref, cid_ref, rank_ref, pos_ref, target_ref, digits_ref, *, flips, capacity):
    nodes = len(flips)
    rows = cid_ref.shape[1]
    flip = cid_ref[...] ^ me_ref[0]
    slot = jnp.zeros_like(flip)
    for g, value in enumerate(flips):
        slot = jnp.where(flip == value, g, slot)
    chunks = [slice(i, i + LANES) for i in range(0, rows, LANES)]
    members = [membership(slot[:, at], nodes, LANES) for at in chunks]
    ahead = lax.broadcasted_iota(jnp.int32, (LANES, LANES), 0) < lax.broadcasted_iota(
        jnp.int32, (LANES, LANES), 1
    )
    ones = [member.astype(jnp.float32) for member in members]
    within = jnp.dot(
        jnp.concatenate(ones, axis=0).astype(jnp.bfloat16),
        ahead.astype(jnp.float32).astype(jnp.bfloat16),
        preferred_element_type=jnp.float32,
    )
    before = jnp.zeros((nodes, 1), jnp.float32)
    for i, at in enumerate(chunks):
        counts = within[i * nodes : (i + 1) * nodes, :] + before
        pos = jnp.sum(jnp.where(members[i], counts, 0.0), axis=0, keepdims=True).astype(jnp.int32)
        pos_ref[:, at] = pos
        target_ref[:, at] = slot[:, at] * capacity + pos
        before = before + jnp.sum(ones[i], axis=1, keepdims=True)
        shown = rank_ref[:, at] + 1
        digit = lax.broadcasted_iota(jnp.int32, (LANES, LANES), 0)
        digits = jnp.where(
            digit == 0,
            shown & 127,
            jnp.where(digit == 1, (shown >> 7) & 127, jnp.where(digit == 2, (shown >> 14) & 127, 0)),
        ).astype(jnp.float32)
        digits_ref[at, :] = jnp.transpose(digits).astype(jnp.bfloat16)


def pack_kernel(x_ref, target_ref, digits_ref, *out_refs, capacity):
    nodes = len(out_refs)
    rows, width = x_ref.shape
    pieces = width // LANES
    slots = nodes * capacity
    place = lax.broadcasted_iota(jnp.int32, (slots, rows), 0) == target_ref[...]
    place = place.astype(jnp.float32).astype(jnp.bfloat16)
    widened = x_ref[...].astype(jnp.float32)
    squares = jnp.sum(widened * widened, axis=1, keepdims=True)
    normed = (widened * lax.rsqrt(squares + 1e-06)).astype(jnp.bfloat16)
    whole = jnp.concatenate([normed, digits_ref[...]], axis=1)
    moved = jnp.dot(place, whole, preferred_element_type=jnp.float32)
    for first in range(0, slots, LANES):
        lines = jnp.transpose(moved[first : first + LANES, width:])[0:EXTRA, :].astype(jnp.bfloat16)
        for g in range(first // capacity, (first + LANES) // capacity):
            at = g * capacity
            for p in range(pieces):
                out_refs[g][p * capacity : (p + 1) * capacity, :] = moved[
                    at : at + capacity, p * LANES : (p + 1) * LANES
                ].astype(jnp.bfloat16)
            out_refs[g][pieces * capacity :, :] = jnp.zeros((EXTRA, LANES), jnp.bfloat16)
            out_refs[g][pieces * capacity :, 0:capacity] = lines[:, at - first : at - first + capacity]


def assemble_kernel(*refs, messages, capacity, pieces):
    sources, (rows_ref, line_ref) = refs[:messages], refs[-2:]
    if len(sources[0].shape) == 3:
        sources = [sources[0].at[i] for i in range(sources[0].shape[0])]
    for i, source in enumerate(sources):
        for p in range(pieces):
            rows_ref[i * capacity : (i + 1) * capacity, p * LANES : (p + 1) * LANES] = source[
                p * capacity : (p + 1) * capacity, :
            ]
        tile = source[pieces * capacity :, :].astype(jnp.float32)
        square = jnp.concatenate([tile, jnp.zeros((LANES - EXTRA, LANES), jnp.float32)], axis=0)
        rows_ref[i * capacity : (i + 1) * capacity, pieces * LANES :] = jnp.transpose(square)[
            0:capacity, :
        ].astype(jnp.bfloat16)
        line = tile[0:1, :] + 128.0 * tile[1:2, :] + 16384.0 * tile[2:3, :]
        line_ref[0:1, i * capacity : (i + 1) * capacity] = line[:, 0:capacity]


def assemble(messages, count, after, held, width):
    pieces = width // LANES
    capacity = (messages[0].shape[-2] - EXTRA) // pieces
    rows = count * capacity
    ahead = len(messages) + len(after)
    return pl.pallas_call(
        functools.partial(assemble_kernel, messages=len(messages), capacity=capacity, pieces=pieces),
        out_shape=[jax.ShapeDtypeStruct(h.shape, h.dtype) for h in held]
        + [
            jax.ShapeDtypeStruct((rows, width + LANES), jnp.bfloat16),
            jax.ShapeDtypeStruct((8, rows), jnp.float32),
        ],
        in_specs=[VMEM] * len(messages) + [ANY] * (len(after) + len(held)),
        out_specs=[ANY] * len(held) + [VMEM, VMEM],
        input_output_aliases={ahead + i: i for i in range(len(held))},
        compiler_params=PARAMS,
        cost_estimate=LIGHT,
    )(*messages, *after, *held)


def match_kernel(*refs, width, queries, candidates, pairs, mirrored, carried):
    q_refs, refs = refs[:queries], refs[queries:]
    line_refs, refs = refs[:queries], refs[queries:]
    k_refs, refs = refs[:candidates], refs[candidates:]
    carry_refs, out_refs = dict(zip(carried, refs)), refs[len(carried) :]
    best = {}
    for q in range(queries):
        rows = q_refs[q].shape[0]
        best[q] = carry_refs[q][0:1, :] if q in carry_refs else jnp.full((1, rows), -1.0, jnp.float32)
    for k in range(candidates):
        for first in range(0, k_refs[k].shape[0], TILE):
            at = slice(first, min(first + TILE, k_refs[k].shape[0]))
            tile = k_refs[k][at, width:].astype(jnp.float32)
            theirs = tile[:, 0:1] + 128.0 * tile[:, 1:2] + 16384.0 * tile[:, 2:3]
            other = jnp.where(theirs > 0.0, theirs, NEVER)
            for q in range(queries):
                if (q, k) not in pairs:
                    continue
                scores = lax.dot_general(
                    k_refs[k][at, 0:width],
                    q_refs[q][:, 0:width],
                    (((1,), (1,)), ((), ())),
                    preferred_element_type=jnp.float32,
                )
                kept = jnp.where(other < line_refs[q][0:1, :], scores, -1.0)
                best[q] = jnp.maximum(best[q], jnp.max(kept, axis=0, keepdims=True))
                if (q, k) in mirrored:
                    asked = mirrored[q, k]
                    line = line_refs[q][0:1, :]
                    line = jnp.where(line > 0.0, line, NEVER)
                    kept = jnp.where(line < theirs, scores, -1.0)
                    folded = kept[:, 0:LANES]
                    for lane in range(LANES, kept.shape[1], LANES):
                        folded = jnp.maximum(folded, kept[:, lane : lane + LANES])
                    found = jnp.max(jnp.transpose(folded), axis=0, keepdims=True)
                    best[asked] = jnp.maximum(best[asked], found)
    for q in range(queries):
        out_refs[q][0:1, :] = best[q]


def match(groups, candidates, pairs, carry, width, mirrored=None):
    carried = tuple(sorted(carry))
    operands = [
        *[rows for rows, _ in groups],
        *[line for _, line in groups],
        *candidates,
        *[carry[q] for q in carried],
    ]
    return pl.pallas_call(
        functools.partial(
            match_kernel,
            width=width,
            queries=len(groups),
            candidates=len(candidates),
            pairs=frozenset(pairs),
            mirrored=mirrored or {},
            carried=carried,
        ),
        out_shape=[jax.ShapeDtypeStruct(line.shape, jnp.float32) for _, line in groups],
        in_specs=[VMEM] * len(operands),
        out_specs=[VMEM] * len(groups),
        compiler_params=PARAMS,
        cost_estimate=LIGHT,
    )(*operands)


def address_kernel(me_ref, *refs, flips, capacity):
    *lines, out_ref = refs
    out_ref[...] = jnp.zeros(out_ref.shape, jnp.float32)
    blocks = [(line, i) for line in lines for i in range(line.shape[1] // capacity)]
    for flip, (line, i) in zip(flips, blocks):
        out_ref[(out_ref.shape[0] - 1) - (me_ref[0] ^ flip), 0:1, 0:capacity] = line[0:1, i * capacity : (i + 1) * capacity]


def unpack_kernel(back_ref, cid_ref, pos_ref, out_ref):
    nodes = back_ref.shape[0]
    lines = jnp.concatenate([back_ref[g] for g in range(nodes)], axis=0)
    for first in range(0, cid_ref.shape[1], LANES):
        at = slice(first, first + LANES)
        index = jnp.broadcast_to(pos_ref[:, at], (nodes, LANES))
        found = jnp.take_along_axis(lines, index, axis=1, mode="promise_in_bounds")
        member = membership((nodes - 1) - cid_ref[:, at], nodes, LANES)
        out_ref[:, at] = jnp.sum(jnp.where(member, found, 0.0), axis=0, keepdims=True)


def body(embeddings, cluster_id, rank):
    nodes = lax.axis_size("ingest")
    rows, width = embeddings.shape
    capacity = 2 * rows // nodes
    height = capacity * (width // LANES) + EXTRA
    cid = cluster_id.reshape(1, rows)
    half = nodes // 2
    me = lax.axis_index("ingest").astype(jnp.int32).reshape(1)
    flips = partners(nodes)
    pos, target, digits = pl.pallas_call(
        functools.partial(place_kernel, flips=flips, capacity=capacity),
        out_shape=(
            jax.ShapeDtypeStruct((1, rows), jnp.int32),
            jax.ShapeDtypeStruct((1, rows), jnp.int32),
            jax.ShapeDtypeStruct((rows, LANES), jnp.bfloat16),
        ),
        in_specs=[SMEM] + [VMEM] * 2,
        out_specs=[VMEM] * 3,
        compiler_params=PARAMS,
        cost_estimate=pl.CostEstimate(flops=2**28, bytes_accessed=2**12, transcendentals=0),
    )(me, cid, rank.reshape(1, rows))
    messages = pl.pallas_call(
        functools.partial(pack_kernel, capacity=capacity),
        out_shape=[jax.ShapeDtypeStruct((height, LANES), jnp.bfloat16)] * nodes,
        in_specs=[VMEM] * 3,
        out_specs=[VMEM] * nodes,
        compiler_params=PARAMS,
        cost_estimate=pl.CostEstimate(
            flops=2 * nodes * capacity * rows * (width + LANES), bytes_accessed=2**12, transcendentals=0
        ),
    )(embeddings, target, digits)
    messages = list(messages)
    for g in range(1, nodes):
        messages[g] = lax.ppermute(messages[g], "ingest", [(i, i ^ flips[g]) for i in range(nodes)])

    def across(rows):
        return lax.ppermute(rows, "span", [(0, 1), (1, 0)])

    b, b_line = assemble(messages[half:], half, [], [], width)
    (best_b,) = match([(b, b_line)], [b], [(0, 0)], {}, width)
    a, a_line = assemble(messages[:half], half, [best_b], [], width)
    groups = [(a, a_line), (b, b_line)]
    best_a, best_b = match(
        groups, [b, a], [(0, 1), (0, 0)], {1: best_b}, width, mirrored={(0, 0): 1}
    )
    for other in (across(b), across(a)):
        best_a, best_b = match(groups, [other], [(0, 0), (1, 0)], {0: best_a, 1: best_b}, width)
    highest = pl.pallas_call(
        functools.partial(address_kernel, flips=flips, capacity=capacity),
        out_shape=jax.ShapeDtypeStruct((nodes, 1, LANES), jnp.float32),
        in_specs=[SMEM] + [VMEM] * 2,
        out_specs=VMEM,
        compiler_params=PARAMS,
    )(me, best_a, best_b)
    back = lax.all_to_all(
        highest,
        "ingest",
        split_axis=0,
        concat_axis=0,
        tiled=True,
        axis_index_groups=[list(range(nodes))[::-1]],
    )
    result = pl.pallas_call(
        unpack_kernel,
        out_shape=jax.ShapeDtypeStruct((1, rows), jnp.float32),
        in_specs=[VMEM] * 3,
        out_specs=VMEM,
        compiler_params=PARAMS,
    )(back, cid, pos)
    return result.reshape(rows)


def solution(mesh):
    in_specs = (P(("ingest", "span"), None), P(("ingest", "span")), P(("ingest", "span")))
    out_specs = P(("ingest", "span"))
    return jax.shard_map(body, mesh=mesh, in_specs=in_specs, out_specs=out_specs, check_vma=False)
```

```python
import functools

import jax
import jax.numpy as jnp
from jax import lax
from jax.experimental import pallas as pl
from jax.experimental.pallas import tpu as pltpu
from jax.sharding import PartitionSpec as P

LANES = 128
EXTRA = 8
NEVER = 2.0**24
TILE = 512
PARAMS = pltpu.CompilerParams(vmem_limit_bytes=40 * 2**20)
VMEM = pl.BlockSpec(memory_space=pltpu.VMEM)
SMEM = pl.BlockSpec(memory_space=pltpu.SMEM)
ANY = pl.BlockSpec(memory_space=pl.ANY)


LIGHT = pl.CostEstimate(flops=1, bytes_accessed=1, transcendentals=0)


def membership(cid, nodes, rows):
    return lax.broadcasted_iota(jnp.int32, (nodes, rows), 0) == cid


def partners(nodes):
    half = nodes // 2
    quarter = half // 2
    far = [flip for i in range(quarter) for flip in (half + quarter + i, half + i)]
    near = [*range(quarter, half), *range(1, quarter)]
    sequence = [far[0]]
    for pair in zip(near, far[1:]):
        sequence.extend(pair)
    flips = [0] * nodes
    for g, flip in zip([*range(half + 3, nodes), *range(half, half + 3), *range(1, half)], sequence):
        flips[g] = flip
    return flips


def place_kernel(me_ref, cid_ref, rank_ref, pos_ref, target_ref, digits_ref, *, flips, capacity):
    nodes = len(flips)
    rows = cid_ref.shape[1]
    flip = cid_ref[...] ^ me_ref[0]
    slot = jnp.zeros_like(flip)
    for g, value in enumerate(flips):
        slot = jnp.where(flip == value, g, slot)
    chunks = [slice(i, i + LANES) for i in range(0, rows, LANES)]
    members = [membership(slot[:, at], nodes, LANES) for at in chunks]
    ahead = lax.broadcasted_iota(jnp.int32, (LANES, LANES), 0) < lax.broadcasted_iota(
        jnp.int32, (LANES, LANES), 1
    )
    ones = [member.astype(jnp.float32) for member in members]
    within = jnp.dot(
        jnp.concatenate(ones, axis=0).astype(jnp.bfloat16),
        ahead.astype(jnp.float32).astype(jnp.bfloat16),
        preferred_element_type=jnp.float32,
    )
    before = jnp.zeros((nodes, 1), jnp.float32)
    for i, at in enumerate(chunks):
        counts = within[i * nodes : (i + 1) * nodes, :] + before
        pos = jnp.sum(jnp.where(members[i], counts, 0.0), axis=0, keepdims=True).astype(jnp.int32)
        pos_ref[:, at] = pos
        target_ref[:, at] = slot[:, at] * capacity + pos
        before = before + jnp.sum(ones[i], axis=1, keepdims=True)
        shown = rank_ref[:, at] + 1
        digit = lax.broadcasted_iota(jnp.int32, (LANES, LANES), 0)
        digits = jnp.where(
            digit == 0,
            shown & 127,
            jnp.where(digit == 1, (shown >> 7) & 127, jnp.where(digit == 2, (shown >> 14) & 127, 0)),
        ).astype(jnp.float32)
        digits_ref[at, :] = jnp.transpose(digits).astype(jnp.bfloat16)


def pack_kernel(rows_ref, target_ref, digits_ref, *refs, chosen, capacity, first):
    *out_refs, whole_ref = refs if first else (*refs, None)
    rows = rows_ref.shape[0]
    slot = lax.broadcasted_iota(jnp.int32, (capacity, rows), 0)
    place = [(slot + g * capacity == target_ref[...]).astype(jnp.float32) for g in chosen]
    place = jnp.concatenate(place, axis=0).astype(jnp.bfloat16)
    if first:
        widened = rows_ref[...].astype(jnp.float32)
        squares = jnp.sum(widened * widened, axis=1, keepdims=True)
        normed = (widened * lax.rsqrt(squares + 1e-06)).astype(jnp.bfloat16)
        whole = jnp.concatenate([normed, digits_ref[...]], axis=1)
        whole_ref[...] = whole
    else:
        whole = rows_ref[...]
    width = whole.shape[1] - LANES
    pieces = width // LANES
    moved = jnp.dot(place, whole, preferred_element_type=jnp.float32)
    for i, out_ref in enumerate(out_refs):
        at = slice(i * capacity, (i + 1) * capacity)
        for p in range(pieces):
            out_ref[p * capacity : (p + 1) * capacity, :] = moved[
                at, p * LANES : (p + 1) * LANES
            ].astype(jnp.bfloat16)
        square = jnp.concatenate(
            [moved[at, width:], jnp.zeros((LANES - capacity, LANES), jnp.float32)], axis=0
        )
        out_ref[pieces * capacity :, :] = jnp.transpose(square)[0:EXTRA, :].astype(jnp.bfloat16)


def assemble_kernel(*refs, messages, capacity, pieces):
    sources, (rows_ref, line_ref) = refs[:messages], refs[-2:]
    if len(sources[0].shape) == 3:
        sources = [sources[0].at[i] for i in range(sources[0].shape[0])]
    for i, source in enumerate(sources):
        for p in range(pieces):
            rows_ref[i * capacity : (i + 1) * capacity, p * LANES : (p + 1) * LANES] = source[
                p * capacity : (p + 1) * capacity, :
            ]
        tile = source[pieces * capacity :, :].astype(jnp.float32)
        square = jnp.concatenate([tile, jnp.zeros((LANES - EXTRA, LANES), jnp.float32)], axis=0)
        rows_ref[i * capacity : (i + 1) * capacity, pieces * LANES :] = jnp.transpose(square)[
            0:capacity, :
        ].astype(jnp.bfloat16)
        line = tile[0:1, :] + 128.0 * tile[1:2, :] + 16384.0 * tile[2:3, :]
        line_ref[0:1, i * capacity : (i + 1) * capacity] = line[:, 0:capacity]


def assemble(messages, count, after, held, width):
    pieces = width // LANES
    capacity = (messages[0].shape[-2] - EXTRA) // pieces
    rows = count * capacity
    ahead = len(messages) + len(after)
    return pl.pallas_call(
        functools.partial(assemble_kernel, messages=len(messages), capacity=capacity, pieces=pieces),
        out_shape=[jax.ShapeDtypeStruct(h.shape, h.dtype) for h in held]
        + [
            jax.ShapeDtypeStruct((rows, width + LANES), jnp.bfloat16),
            jax.ShapeDtypeStruct((8, rows), jnp.float32),
        ],
        in_specs=[VMEM] * len(messages) + [ANY] * (len(after) + len(held)),
        out_specs=[ANY] * len(held) + [VMEM, VMEM],
        input_output_aliases={ahead + i: i for i in range(len(held))},
        compiler_params=PARAMS,
        cost_estimate=LIGHT,
    )(*messages, *after, *held)


def match_kernel(*refs, width, queries, candidates, foreign, pairs, mirrored, carried):
    q_refs, refs = refs[:queries], refs[queries:]
    line_refs, refs = refs[:queries], refs[queries:]
    k_refs, refs = refs[:candidates], refs[candidates:]
    carry_refs, out_refs = dict(zip(carried, refs)), refs[len(carried) :]
    best = {}
    for q in range(queries):
        rows = q_refs[q].shape[0]
        best[q] = carry_refs[q][0:1, :] if q in carry_refs else jnp.full((1, rows), -1.0, jnp.float32)
    for extra in range(queries, queries + foreign):
        best[extra] = jnp.full((1, out_refs[extra].shape[1]), -1.0, jnp.float32)
    for k in range(candidates):
        for first in range(0, k_refs[k].shape[0], TILE):
            at = slice(first, min(first + TILE, k_refs[k].shape[0]))
            tile = k_refs[k][at, width:].astype(jnp.float32)
            theirs = tile[:, 0:1] + 128.0 * tile[:, 1:2] + 16384.0 * tile[:, 2:3]
            other = jnp.where(theirs > 0.0, theirs, NEVER)
            for q in range(queries):
                if (q, k) not in pairs:
                    continue
                scores = lax.dot_general(
                    k_refs[k][at, 0:width],
                    q_refs[q][:, 0:width],
                    (((1,), (1,)), ((), ())),
                    preferred_element_type=jnp.float32,
                )
                kept = jnp.where(other < line_refs[q][0:1, :], scores, -1.0)
                best[q] = jnp.maximum(best[q], jnp.max(kept, axis=0, keepdims=True))
                if (q, k) in mirrored:
                    asked = mirrored[q, k]
                    line = line_refs[q][0:1, :]
                    line = jnp.where(line > 0.0, line, NEVER)
                    kept = jnp.where(line < theirs, scores, -1.0)
                    folded = kept[:, 0:LANES]
                    for lane in range(LANES, kept.shape[1], LANES):
                        folded = jnp.maximum(folded, kept[:, lane : lane + LANES])
                    found = jnp.max(jnp.transpose(folded), axis=0, keepdims=True)
                    best[asked] = jnp.maximum(best[asked], found)
    for q in range(queries + foreign):
        out_refs[q][0:1, :] = best[q]


def match(groups, candidates, pairs, carry, width, mirrored=None, foreign=0):
    carried = tuple(sorted(carry))
    operands = [
        *[rows for rows, _ in groups],
        *[line for _, line in groups],
        *candidates,
        *[carry[q] for q in carried],
    ]
    return pl.pallas_call(
        functools.partial(
            match_kernel,
            width=width,
            queries=len(groups),
            candidates=len(candidates),
            foreign=foreign,
            pairs=frozenset(pairs),
            mirrored=mirrored or {},
            carried=carried,
        ),
        out_shape=[jax.ShapeDtypeStruct(line.shape, jnp.float32) for _, line in groups]
        + [jax.ShapeDtypeStruct(groups[0][1].shape, jnp.float32)] * foreign,
        in_specs=[VMEM] * len(operands),
        out_specs=[VMEM] * (len(groups) + foreign),
        compiler_params=PARAMS,
        cost_estimate=LIGHT,
    )(*operands)


def address_kernel(me_ref, first_ref, second_ref, other_ref, out_ref, *, flips, capacity):
    out_ref[...] = jnp.zeros(out_ref.shape, jnp.float32)
    second = jnp.maximum(second_ref[0:1, :], other_ref[0:1, :])
    lines = [first_ref[0:1, :], second]
    blocks = [(line, i) for line in lines for i in range(line.shape[1] // capacity)]
    for flip, (line, i) in zip(flips, blocks):
        out_ref[(out_ref.shape[0] - 1) - (me_ref[0] ^ flip), 0:1, 0:capacity] = line[
            :, i * capacity : (i + 1) * capacity
        ]


def unpack_kernel(back_ref, cid_ref, pos_ref, out_ref):
    nodes = back_ref.shape[0]
    lines = jnp.concatenate([back_ref[g] for g in range(nodes)], axis=0)
    for first in range(0, cid_ref.shape[1], LANES):
        at = slice(first, first + LANES)
        index = jnp.broadcast_to(pos_ref[:, at], (nodes, LANES))
        found = jnp.take_along_axis(lines, index, axis=1, mode="promise_in_bounds")
        member = membership((nodes - 1) - cid_ref[:, at], nodes, LANES)
        out_ref[:, at] = jnp.sum(jnp.where(member, found, 0.0), axis=0, keepdims=True)


def body(embeddings, cluster_id, rank):
    nodes = lax.axis_size("ingest")
    rows, width = embeddings.shape
    capacity = 2 * rows // nodes
    height = capacity * (width // LANES) + EXTRA
    cid = cluster_id.reshape(1, rows)
    half = nodes // 2
    me = lax.axis_index("ingest").astype(jnp.int32).reshape(1)
    flips = partners(nodes)
    pos, target, digits = pl.pallas_call(
        functools.partial(place_kernel, flips=flips, capacity=capacity),
        out_shape=(
            jax.ShapeDtypeStruct((1, rows), jnp.int32),
            jax.ShapeDtypeStruct((1, rows), jnp.int32),
            jax.ShapeDtypeStruct((rows, LANES), jnp.bfloat16),
        ),
        in_specs=[SMEM] + [VMEM] * 2,
        out_specs=[VMEM] * 3,
        compiler_params=PARAMS,
        cost_estimate=pl.CostEstimate(flops=2**28, bytes_accessed=2**12, transcendentals=0),
    )(me, cid, rank.reshape(1, rows))
    early = range(half, nodes)
    messages = [None] * nodes
    given = embeddings
    for chosen in (list(early), [g for g in range(nodes) if g not in early]):
        first = given is embeddings
        packed = pl.pallas_call(
            functools.partial(pack_kernel, chosen=chosen, capacity=capacity, first=first),
            out_shape=[jax.ShapeDtypeStruct((height, LANES), jnp.bfloat16)] * len(chosen)
            + [jax.ShapeDtypeStruct((rows, width + LANES), jnp.bfloat16)] * first,
            in_specs=[VMEM] * 3,
            out_specs=[VMEM] * (len(chosen) + first),
            compiler_params=PARAMS,
            cost_estimate=pl.CostEstimate(
                flops=2 * len(chosen) * capacity * rows * (width + LANES),
                bytes_accessed=2**12,
                transcendentals=0,
            ),
        )(given, target, digits)
        for g, message in zip(chosen, packed):
            messages[g] = message
        given = packed[-1]
    for g in range(1, nodes):
        messages[g] = lax.ppermute(messages[g], "ingest", [(i, i ^ flips[g]) for i in range(nodes)])

    def across(rows):
        return lax.ppermute(rows, "span", [(0, 1), (1, 0)])

    b, b_line = assemble(messages[half:], half, [], [], width)
    (best_b,) = match([(b, b_line)], [b], [(0, 0)], {}, width)
    a, a_line = assemble(messages[:half], half, [best_b], [], width)
    groups = [(a, a_line), (b, b_line)]
    b_other = across(b)
    best_a, for_other = match([(a, a_line)], [b_other], [(0, 0)], {}, width, {(0, 0): 1}, foreign=1)
    from_other = across(for_other)
    best_a, best_b = match(
        groups,
        [b, a, b_other],
        [(0, 1), (0, 0), (1, 2)],
        {0: best_a, 1: best_b},
        width,
        {(0, 0): 1},
    )
    (best_a,) = match([(a, a_line)], [across(a)], [(0, 0)], {0: best_a}, width)
    highest = pl.pallas_call(
        functools.partial(address_kernel, flips=flips, capacity=capacity),
        out_shape=jax.ShapeDtypeStruct((nodes, 1, LANES), jnp.float32),
        in_specs=[SMEM] + [VMEM] * 3,
        out_specs=VMEM,
        compiler_params=PARAMS,
    )(me, best_a, best_b, from_other)
    back = lax.all_to_all(
        highest,
        "ingest",
        split_axis=0,
        concat_axis=0,
        tiled=True,
        axis_index_groups=[list(range(nodes))[::-1]],
    )
    result = pl.pallas_call(
        unpack_kernel,
        out_shape=jax.ShapeDtypeStruct((1, rows), jnp.float32),
        in_specs=[VMEM] * 3,
        out_specs=VMEM,
        compiler_params=PARAMS,
    )(back, cid, pos)
    return result.reshape(rows)


def solution(mesh):
    in_specs = (P(("ingest", "span"), None), P(("ingest", "span")), P(("ingest", "span")))
    out_specs = P(("ingest", "span"))
    return jax.shard_map(body, mesh=mesh, in_specs=in_specs, out_specs=out_specs, check_vma=False)
```

```python
import functools

import jax
import jax.numpy as jnp
from jax import lax
from jax.experimental import pallas as pl
from jax.experimental.pallas import tpu as pltpu
from jax.sharding import PartitionSpec as P

LANES = 128
EXTRA = 8
NEVER = 2.0**24
TILE = 512
PARAMS = pltpu.CompilerParams(vmem_limit_bytes=40 * 2**20)
VMEM = pl.BlockSpec(memory_space=pltpu.VMEM)
SMEM = pl.BlockSpec(memory_space=pltpu.SMEM)
ANY = pl.BlockSpec(memory_space=pl.ANY)


LIGHT = pl.CostEstimate(flops=1, bytes_accessed=1, transcendentals=0)


def membership(cid, nodes, rows):
    return lax.broadcasted_iota(jnp.int32, (nodes, rows), 0) == cid


def partners(nodes):
    half = nodes // 2
    quarter = half // 2
    far = [*range(half + quarter, nodes), *range(half, half + quarter)]
    near = [*range(quarter, half), *range(1, quarter)]
    sequence = [far[0]]
    for pair in zip(near, far[1:]):
        sequence.extend(pair)
    flips = [0] * nodes
    for g, flip in zip([*range(half + 3, nodes), *range(half, half + 3), *range(1, half)], sequence):
        flips[g] = flip
    return flips


def place_kernel(me_ref, cid_ref, rank_ref, pos_ref, target_ref, digits_ref, *, flips, capacity):
    nodes = len(flips)
    rows = cid_ref.shape[1]
    flip = cid_ref[...] ^ me_ref[0]
    slot = jnp.zeros_like(flip)
    for g, value in enumerate(flips):
        slot = jnp.where(flip == value, g, slot)
    chunks = [slice(i, i + LANES) for i in range(0, rows, LANES)]
    members = [membership(slot[:, at], nodes, LANES) for at in chunks]
    ahead = lax.broadcasted_iota(jnp.int32, (LANES, LANES), 0) < lax.broadcasted_iota(
        jnp.int32, (LANES, LANES), 1
    )
    ones = [member.astype(jnp.float32) for member in members]
    within = jnp.dot(
        jnp.concatenate(ones, axis=0).astype(jnp.bfloat16),
        ahead.astype(jnp.float32).astype(jnp.bfloat16),
        preferred_element_type=jnp.float32,
    )
    before = jnp.zeros((nodes, 1), jnp.float32)
    for i, at in enumerate(chunks):
        counts = within[i * nodes : (i + 1) * nodes, :] + before
        pos = jnp.sum(jnp.where(members[i], counts, 0.0), axis=0, keepdims=True).astype(jnp.int32)
        pos_ref[:, at] = pos
        target_ref[:, at] = slot[:, at] * capacity + pos
        before = before + jnp.sum(ones[i], axis=1, keepdims=True)
        shown = rank_ref[:, at] + 1
        digit = lax.broadcasted_iota(jnp.int32, (LANES, LANES), 0)
        digits = jnp.where(
            digit == 0,
            shown & 127,
            jnp.where(digit == 1, (shown >> 7) & 127, jnp.where(digit == 2, (shown >> 14) & 127, 0)),
        ).astype(jnp.float32)
        digits_ref[at, :] = jnp.transpose(digits).astype(jnp.bfloat16)


def pack_kernel(rows_ref, target_ref, digits_ref, *refs, chosen, capacity, first):
    *out_refs, whole_ref = refs if first else (*refs, None)
    rows = rows_ref.shape[0]
    slot = lax.broadcasted_iota(jnp.int32, (capacity, rows), 0)
    place = [(slot + g * capacity == target_ref[...]).astype(jnp.float32) for g in chosen]
    place = jnp.concatenate(place, axis=0).astype(jnp.bfloat16)
    if first:
        widened = rows_ref[...].astype(jnp.float32)
        squares = jnp.sum(widened * widened, axis=1, keepdims=True)
        normed = (widened * lax.rsqrt(squares + 1e-06)).astype(jnp.bfloat16)
        whole = jnp.concatenate([normed, digits_ref[...]], axis=1)
        whole_ref[...] = whole
    else:
        whole = rows_ref[...]
    width = whole.shape[1] - LANES
    pieces = width // LANES
    moved = jnp.dot(place, whole, preferred_element_type=jnp.float32)
    for i, out_ref in enumerate(out_refs):
        at = slice(i * capacity, (i + 1) * capacity)
        for p in range(pieces):
            out_ref[p * capacity : (p + 1) * capacity, :] = moved[
                at, p * LANES : (p + 1) * LANES
            ].astype(jnp.bfloat16)
        square = jnp.concatenate(
            [moved[at, width:], jnp.zeros((LANES - capacity, LANES), jnp.float32)], axis=0
        )
        out_ref[pieces * capacity :, :] = jnp.transpose(square)[0:EXTRA, :].astype(jnp.bfloat16)


def assemble_kernel(*refs, messages, capacity, pieces):
    sources, (rows_ref, line_ref) = refs[:messages], refs[-2:]
    if len(sources[0].shape) == 3:
        sources = [sources[0].at[i] for i in range(sources[0].shape[0])]
    for i, source in enumerate(sources):
        for p in range(pieces):
            rows_ref[i * capacity : (i + 1) * capacity, p * LANES : (p + 1) * LANES] = source[
                p * capacity : (p + 1) * capacity, :
            ]
        tile = source[pieces * capacity :, :].astype(jnp.float32)
        square = jnp.concatenate([tile, jnp.zeros((LANES - EXTRA, LANES), jnp.float32)], axis=0)
        rows_ref[i * capacity : (i + 1) * capacity, pieces * LANES :] = jnp.transpose(square)[
            0:capacity, :
        ].astype(jnp.bfloat16)
        line = tile[0:1, :] + 128.0 * tile[1:2, :] + 16384.0 * tile[2:3, :]
        line_ref[0:1, i * capacity : (i + 1) * capacity] = line[:, 0:capacity]


def assemble(messages, count, after, held, width):
    pieces = width // LANES
    capacity = (messages[0].shape[-2] - EXTRA) // pieces
    rows = count * capacity
    ahead = len(messages) + len(after)
    return pl.pallas_call(
        functools.partial(assemble_kernel, messages=len(messages), capacity=capacity, pieces=pieces),
        out_shape=[jax.ShapeDtypeStruct(h.shape, h.dtype) for h in held]
        + [
            jax.ShapeDtypeStruct((rows, width + LANES), jnp.bfloat16),
            jax.ShapeDtypeStruct((8, rows), jnp.float32),
        ],
        in_specs=[VMEM] * len(messages) + [ANY] * (len(after) + len(held)),
        out_specs=[ANY] * len(held) + [VMEM, VMEM],
        input_output_aliases={ahead + i: i for i in range(len(held))},
        compiler_params=PARAMS,
        cost_estimate=LIGHT,
    )(*messages, *after, *held)


def match_kernel(*refs, width, queries, candidates, foreign, pairs, mirrored, carried):
    q_refs, refs = refs[:queries], refs[queries:]
    line_refs, refs = refs[:queries], refs[queries:]
    k_refs, refs = refs[:candidates], refs[candidates:]
    carry_refs, out_refs = dict(zip(carried, refs)), refs[len(carried) :]
    best = {}
    for q in range(queries):
        rows = q_refs[q].shape[0]
        best[q] = carry_refs[q][0:1, :] if q in carry_refs else jnp.full((1, rows), -1.0, jnp.float32)
    for extra in range(queries, queries + foreign):
        best[extra] = jnp.full((1, out_refs[extra].shape[1]), -1.0, jnp.float32)
    for k in range(candidates):
        for first in range(0, k_refs[k].shape[0], TILE):
            at = slice(first, min(first + TILE, k_refs[k].shape[0]))
            tile = k_refs[k][at, width:].astype(jnp.float32)
            theirs = tile[:, 0:1] + 128.0 * tile[:, 1:2] + 16384.0 * tile[:, 2:3]
            other = jnp.where(theirs > 0.0, theirs, NEVER)
            for q in range(queries):
                if (q, k) not in pairs:
                    continue
                scores = lax.dot_general(
                    k_refs[k][at, 0:width],
                    q_refs[q][:, 0:width],
                    (((1,), (1,)), ((), ())),
                    preferred_element_type=jnp.float32,
                )
                kept = jnp.where(other < line_refs[q][0:1, :], scores, -1.0)
                best[q] = jnp.maximum(best[q], jnp.max(kept, axis=0, keepdims=True))
                if (q, k) in mirrored:
                    asked = mirrored[q, k]
                    line = line_refs[q][0:1, :]
                    line = jnp.where(line > 0.0, line, NEVER)
                    kept = jnp.where(line < theirs, scores, -1.0)
                    folded = kept[:, 0:LANES]
                    for lane in range(LANES, kept.shape[1], LANES):
                        folded = jnp.maximum(folded, kept[:, lane : lane + LANES])
                    found = jnp.max(jnp.transpose(folded), axis=0, keepdims=True)
                    best[asked] = jnp.maximum(best[asked], found)
    for q in range(queries + foreign):
        out_refs[q][0:1, :] = best[q]


def match(groups, candidates, pairs, carry, width, mirrored=None, foreign=0):
    carried = tuple(sorted(carry))
    operands = [
        *[rows for rows, _ in groups],
        *[line for _, line in groups],
        *candidates,
        *[carry[q] for q in carried],
    ]
    return pl.pallas_call(
        functools.partial(
            match_kernel,
            width=width,
            queries=len(groups),
            candidates=len(candidates),
            foreign=foreign,
            pairs=frozenset(pairs),
            mirrored=mirrored or {},
            carried=carried,
        ),
        out_shape=[jax.ShapeDtypeStruct(line.shape, jnp.float32) for _, line in groups]
        + [jax.ShapeDtypeStruct(groups[0][1].shape, jnp.float32)] * foreign,
        in_specs=[VMEM] * len(operands),
        out_specs=[VMEM] * (len(groups) + foreign),
        compiler_params=PARAMS,
        cost_estimate=LIGHT,
    )(*operands)


def address_kernel(me_ref, first_ref, second_ref, other_ref, out_ref, *, flips, capacity):
    out_ref[...] = jnp.zeros(out_ref.shape, jnp.float32)
    second = jnp.maximum(second_ref[0:1, :], other_ref[0:1, :])
    lines = [first_ref[0:1, :], second]
    blocks = [(line, i) for line in lines for i in range(line.shape[1] // capacity)]
    for flip, (line, i) in zip(flips, blocks):
        out_ref[(out_ref.shape[0] - 1) - (me_ref[0] ^ flip), 0:1, 0:capacity] = line[
            :, i * capacity : (i + 1) * capacity
        ]


def unpack_kernel(back_ref, cid_ref, pos_ref, out_ref):
    nodes = back_ref.shape[0]
    lines = jnp.concatenate([back_ref[g] for g in range(nodes)], axis=0)
    for first in range(0, cid_ref.shape[1], LANES):
        at = slice(first, first + LANES)
        index = jnp.broadcast_to(pos_ref[:, at], (nodes, LANES))
        found = jnp.take_along_axis(lines, index, axis=1, mode="promise_in_bounds")
        member = membership((nodes - 1) - cid_ref[:, at], nodes, LANES)
        out_ref[:, at] = jnp.sum(jnp.where(member, found, 0.0), axis=0, keepdims=True)


def body(embeddings, cluster_id, rank):
    nodes = lax.axis_size("ingest")
    rows, width = embeddings.shape
    capacity = 2 * rows // nodes
    height = capacity * (width // LANES) + EXTRA
    cid = cluster_id.reshape(1, rows)
    half = nodes // 2
    me = lax.axis_index("ingest").astype(jnp.int32).reshape(1)
    flips = partners(nodes)
    pos, target, digits = pl.pallas_call(
        functools.partial(place_kernel, flips=flips, capacity=capacity),
        out_shape=(
            jax.ShapeDtypeStruct((1, rows), jnp.int32),
            jax.ShapeDtypeStruct((1, rows), jnp.int32),
            jax.ShapeDtypeStruct((rows, LANES), jnp.bfloat16),
        ),
        in_specs=[SMEM] + [VMEM] * 2,
        out_specs=[VMEM] * 3,
        compiler_params=PARAMS,
        cost_estimate=pl.CostEstimate(flops=2**28, bytes_accessed=2**12, transcendentals=0),
    )(me, cid, rank.reshape(1, rows))
    early = range(half, nodes)
    messages = [None] * nodes
    given = embeddings
    for chosen in (list(early), [g for g in range(nodes) if g not in early]):
        first = given is embeddings
        packed = pl.pallas_call(
            functools.partial(pack_kernel, chosen=chosen, capacity=capacity, first=first),
            out_shape=[jax.ShapeDtypeStruct((height, LANES), jnp.bfloat16)] * len(chosen)
            + [jax.ShapeDtypeStruct((rows, width + LANES), jnp.bfloat16)] * first,
            in_specs=[VMEM] * 3,
            out_specs=[VMEM] * (len(chosen) + first),
            compiler_params=PARAMS,
            cost_estimate=pl.CostEstimate(
                flops=2 * len(chosen) * capacity * rows * (width + LANES),
                bytes_accessed=2**12,
                transcendentals=0,
            ),
        )(given, target, digits)
        for g, message in zip(chosen, packed):
            messages[g] = message
        given = packed[-1]
    for g in range(1, nodes):
        messages[g] = lax.ppermute(messages[g], "ingest", [(i, i ^ flips[g]) for i in range(nodes)])

    def across(rows):
        return lax.ppermute(rows, "span", [(0, 1), (1, 0)])

    b, b_line = assemble(messages[half:], half, [], [], width)
    (best_b,) = match([(b, b_line)], [b], [(0, 0)], {}, width)
    a, a_line = assemble(messages[:half], half, [best_b], [], width)
    groups = [(a, a_line), (b, b_line)]
    b_other = across(b)
    best_a, for_other = match([(a, a_line)], [b_other], [(0, 0)], {}, width, {(0, 0): 1}, foreign=1)
    from_other = across(for_other)
    best_a, best_b = match(
        groups,
        [b, a, b_other],
        [(0, 1), (0, 0), (1, 2)],
        {0: best_a, 1: best_b},
        width,
        {(0, 0): 1},
    )
    (best_a,) = match([(a, a_line)], [across(a)], [(0, 0)], {0: best_a}, width)
    highest = pl.pallas_call(
        functools.partial(address_kernel, flips=flips, capacity=capacity),
        out_shape=jax.ShapeDtypeStruct((nodes, 1, LANES), jnp.float32),
        in_specs=[SMEM] + [VMEM] * 3,
        out_specs=VMEM,
        compiler_params=PARAMS,
    )(me, best_a, best_b, from_other)
    back = lax.all_to_all(
        highest,
        "ingest",
        split_axis=0,
        concat_axis=0,
        tiled=True,
        axis_index_groups=[list(range(nodes))[::-1]],
    )
    result = pl.pallas_call(
        unpack_kernel,
        out_shape=jax.ShapeDtypeStruct((1, rows), jnp.float32),
        in_specs=[VMEM] * 3,
        out_specs=VMEM,
        compiler_params=PARAMS,
    )(back, cid, pos)
    return result.reshape(rows)


def solution(mesh):
    in_specs = (P(("ingest", "span"), None), P(("ingest", "span")), P(("ingest", "span")))
    out_specs = P(("ingest", "span"))
    return jax.shard_map(body, mesh=mesh, in_specs=in_specs, out_specs=out_specs, check_vma=False)
```

```python
import functools

import jax
import jax.numpy as jnp
from jax import lax
from jax.experimental import pallas as pl
from jax.experimental.pallas import tpu as pltpu
from jax.sharding import PartitionSpec as P

LANES = 128
EXTRA = 16
NEVER = 2.0**24
TILE = 512
PARAMS = pltpu.CompilerParams(vmem_limit_bytes=40 * 2**20)
VMEM = pl.BlockSpec(memory_space=pltpu.VMEM)
SMEM = pl.BlockSpec(memory_space=pltpu.SMEM)
ANY = pl.BlockSpec(memory_space=pl.ANY)


LIGHT = pl.CostEstimate(flops=1, bytes_accessed=1, transcendentals=0)


def membership(cid, nodes, rows):
    return lax.broadcasted_iota(jnp.int32, (nodes, rows), 0) == cid


def partners(nodes):
    half = nodes // 2
    quarter = half // 2
    far = [flip for i in range(quarter) for flip in (half + quarter + i, half + i)]
    near = [*range(quarter, half), *range(1, quarter)]
    sequence = [far[0]]
    for pair in zip(near, far[1:]):
        sequence.extend(pair)
    flips = [0] * nodes
    for g, flip in zip([*range(half + 3, nodes), *range(half, half + 3), *range(1, half)], sequence):
        flips[g] = flip
    return flips


def place_kernel(me_ref, cid_ref, rank_ref, pos_ref, target_ref, digits_ref, *, flips, capacity):
    nodes = len(flips)
    rows = cid_ref.shape[1]
    flip = cid_ref[...] ^ me_ref[0]
    slot = jnp.zeros_like(flip)
    for g, value in enumerate(flips):
        slot = jnp.where(flip == value, g, slot)
    chunks = [slice(i, i + LANES) for i in range(0, rows, LANES)]
    members = [membership(slot[:, at], nodes, LANES) for at in chunks]
    ahead = lax.broadcasted_iota(jnp.int32, (LANES, LANES), 0) < lax.broadcasted_iota(
        jnp.int32, (LANES, LANES), 1
    )
    ones = [member.astype(jnp.float32) for member in members]
    within = jnp.dot(
        jnp.concatenate(ones, axis=0).astype(jnp.bfloat16),
        ahead.astype(jnp.float32).astype(jnp.bfloat16),
        preferred_element_type=jnp.float32,
    )
    before = jnp.zeros((nodes, 1), jnp.float32)
    for i, at in enumerate(chunks):
        counts = within[i * nodes : (i + 1) * nodes, :] + before
        pos = jnp.sum(jnp.where(members[i], counts, 0.0), axis=0, keepdims=True).astype(jnp.int32)
        pos_ref[:, at] = pos
        target_ref[:, at] = slot[:, at] * capacity + pos
        before = before + jnp.sum(ones[i], axis=1, keepdims=True)
        shown = rank_ref[:, at] + 1
        digit = lax.broadcasted_iota(jnp.int32, (LANES, LANES), 0)
        digits = jnp.where(
            digit == 0,
            shown & 127,
            jnp.where(digit == 1, (shown >> 7) & 127, jnp.where(digit == 2, (shown >> 14) & 127, 0)),
        ).astype(jnp.float32)
        digits_ref[at, :] = jnp.transpose(digits).astype(jnp.bfloat16)


def pack_kernel(rows_ref, target_ref, digits_ref, *refs, chosen, capacity, first):
    *out_refs, whole_ref = refs if first else (*refs, None)
    rows = rows_ref.shape[0]
    slot = lax.broadcasted_iota(jnp.int32, (capacity, rows), 0)
    place = [(slot + g * capacity == target_ref[...]).astype(jnp.float32) for g in chosen]
    place = jnp.concatenate(place, axis=0).astype(jnp.bfloat16)
    if first:
        widened = rows_ref[...].astype(jnp.float32)
        squares = jnp.sum(widened * widened, axis=1, keepdims=True)
        normed = (widened * lax.rsqrt(squares + 1e-06)).astype(jnp.bfloat16)
        whole = jnp.concatenate([normed, digits_ref[...]], axis=1)
        whole_ref[...] = whole
    else:
        whole = rows_ref[...]
    width = whole.shape[1] - LANES
    pieces = width // LANES
    moved = jnp.dot(place, whole, preferred_element_type=jnp.float32)
    for i, out_ref in enumerate(out_refs):
        at = slice(i * capacity, (i + 1) * capacity)
        for p in range(pieces):
            out_ref[p * capacity : (p + 1) * capacity, :] = moved[
                at, p * LANES : (p + 1) * LANES
            ].astype(jnp.bfloat16)
        square = jnp.concatenate(
            [moved[at, width:], jnp.zeros((LANES - capacity, LANES), jnp.float32)], axis=0
        )
        out_ref[pieces * capacity :, :] = jnp.transpose(square)[0:EXTRA, :].astype(jnp.bfloat16)


def assemble_kernel(*refs, messages, capacity, pieces):
    sources, (rows_ref, line_ref) = refs[:messages], refs[-2:]
    if len(sources[0].shape) == 3:
        sources = [sources[0].at[i] for i in range(sources[0].shape[0])]
    for i, source in enumerate(sources):
        for p in range(pieces):
            rows_ref[i * capacity : (i + 1) * capacity, p * LANES : (p + 1) * LANES] = source[
                p * capacity : (p + 1) * capacity, :
            ]
        tile = source[pieces * capacity :, :].astype(jnp.float32)
        square = jnp.concatenate([tile, jnp.zeros((LANES - EXTRA, LANES), jnp.float32)], axis=0)
        rows_ref[i * capacity : (i + 1) * capacity, pieces * LANES :] = jnp.transpose(square)[
            0:capacity, :
        ].astype(jnp.bfloat16)
        line = tile[0:1, :] + 128.0 * tile[1:2, :] + 16384.0 * tile[2:3, :]
        line_ref[0:1, i * capacity : (i + 1) * capacity] = line[:, 0:capacity]


def assemble(messages, count, after, held, width):
    pieces = width // LANES
    capacity = (messages[0].shape[-2] - EXTRA) // pieces
    rows = count * capacity
    ahead = len(messages) + len(after)
    return pl.pallas_call(
        functools.partial(assemble_kernel, messages=len(messages), capacity=capacity, pieces=pieces),
        out_shape=[jax.ShapeDtypeStruct(h.shape, h.dtype) for h in held]
        + [
            jax.ShapeDtypeStruct((rows, width + LANES), jnp.bfloat16),
            jax.ShapeDtypeStruct((8, rows), jnp.float32),
        ],
        in_specs=[VMEM] * len(messages) + [ANY] * (len(after) + len(held)),
        out_specs=[ANY] * len(held) + [VMEM, VMEM],
        input_output_aliases={ahead + i: i for i in range(len(held))},
        compiler_params=PARAMS,
        cost_estimate=LIGHT,
    )(*messages, *after, *held)


def match_kernel(*refs, width, queries, candidates, foreign, pairs, mirrored, carried):
    q_refs, refs = refs[:queries], refs[queries:]
    line_refs, refs = refs[:queries], refs[queries:]
    k_refs, refs = refs[:candidates], refs[candidates:]
    carry_refs, out_refs = dict(zip(carried, refs)), refs[len(carried) :]
    best = {}
    for q in range(queries):
        rows = q_refs[q].shape[0]
        best[q] = carry_refs[q][0:1, :] if q in carry_refs else jnp.full((1, rows), -1.0, jnp.float32)
    for extra in range(queries, queries + foreign):
        best[extra] = jnp.full((1, out_refs[extra].shape[1]), -1.0, jnp.float32)
    for k in range(candidates):
        for first in range(0, k_refs[k].shape[0], TILE):
            at = slice(first, min(first + TILE, k_refs[k].shape[0]))
            tile = k_refs[k][at, width:].astype(jnp.float32)
            theirs = tile[:, 0:1] + 128.0 * tile[:, 1:2] + 16384.0 * tile[:, 2:3]
            other = jnp.where(theirs > 0.0, theirs, NEVER)
            for q in range(queries):
                if (q, k) not in pairs:
                    continue
                scores = lax.dot_general(
                    k_refs[k][at, 0:width],
                    q_refs[q][:, 0:width],
                    (((1,), (1,)), ((), ())),
                    preferred_element_type=jnp.float32,
                )
                kept = jnp.where(other < line_refs[q][0:1, :], scores, -1.0)
                best[q] = jnp.maximum(best[q], jnp.max(kept, axis=0, keepdims=True))
                if (q, k) in mirrored:
                    asked = mirrored[q, k]
                    line = line_refs[q][0:1, :]
                    line = jnp.where(line > 0.0, line, NEVER)
                    kept = jnp.where(line < theirs, scores, -1.0)
                    folded = kept[:, 0:LANES]
                    for lane in range(LANES, kept.shape[1], LANES):
                        folded = jnp.maximum(folded, kept[:, lane : lane + LANES])
                    found = jnp.max(jnp.transpose(folded), axis=0, keepdims=True)
                    best[asked] = jnp.maximum(best[asked], found)
    for q in range(queries + foreign):
        out_refs[q][0:1, :] = best[q]


def match(groups, candidates, pairs, carry, width, mirrored=None, foreign=0):
    carried = tuple(sorted(carry))
    operands = [
        *[rows for rows, _ in groups],
        *[line for _, line in groups],
        *candidates,
        *[carry[q] for q in carried],
    ]
    return pl.pallas_call(
        functools.partial(
            match_kernel,
            width=width,
            queries=len(groups),
            candidates=len(candidates),
            foreign=foreign,
            pairs=frozenset(pairs),
            mirrored=mirrored or {},
            carried=carried,
        ),
        out_shape=[jax.ShapeDtypeStruct(line.shape, jnp.float32) for _, line in groups]
        + [jax.ShapeDtypeStruct(groups[0][1].shape, jnp.float32)] * foreign,
        in_specs=[VMEM] * len(operands),
        out_specs=[VMEM] * (len(groups) + foreign),
        compiler_params=PARAMS,
        cost_estimate=LIGHT,
    )(*operands)


def address_kernel(me_ref, first_ref, second_ref, other_ref, out_ref, *, flips, capacity):
    out_ref[...] = jnp.zeros(out_ref.shape, jnp.float32)
    second = jnp.maximum(second_ref[0:1, :], other_ref[0:1, :])
    lines = [first_ref[0:1, :], second]
    blocks = [(line, i) for line in lines for i in range(line.shape[1] // capacity)]
    for flip, (line, i) in zip(flips, blocks):
        out_ref[(out_ref.shape[0] - 1) - (me_ref[0] ^ flip), 0:1, 0:capacity] = line[
            :, i * capacity : (i + 1) * capacity
        ]


def unpack_kernel(back_ref, cid_ref, pos_ref, out_ref):
    nodes = back_ref.shape[0]
    lines = jnp.concatenate([back_ref[g] for g in range(nodes)], axis=0)
    for first in range(0, cid_ref.shape[1], LANES):
        at = slice(first, first + LANES)
        index = jnp.broadcast_to(pos_ref[:, at], (nodes, LANES))
        found = jnp.take_along_axis(lines, index, axis=1, mode="promise_in_bounds")
        member = membership((nodes - 1) - cid_ref[:, at], nodes, LANES)
        out_ref[:, at] = jnp.sum(jnp.where(member, found, 0.0), axis=0, keepdims=True)


def body(embeddings, cluster_id, rank):
    nodes = lax.axis_size("ingest")
    rows, width = embeddings.shape
    capacity = 2 * rows // nodes
    height = capacity * (width // LANES) + EXTRA
    cid = cluster_id.reshape(1, rows)
    half = nodes // 2
    me = lax.axis_index("ingest").astype(jnp.int32).reshape(1)
    flips = partners(nodes)
    pos, target, digits = pl.pallas_call(
        functools.partial(place_kernel, flips=flips, capacity=capacity),
        out_shape=(
            jax.ShapeDtypeStruct((1, rows), jnp.int32),
            jax.ShapeDtypeStruct((1, rows), jnp.int32),
            jax.ShapeDtypeStruct((rows, LANES), jnp.bfloat16),
        ),
        in_specs=[SMEM] + [VMEM] * 2,
        out_specs=[VMEM] * 3,
        compiler_params=PARAMS,
        cost_estimate=pl.CostEstimate(flops=2**28, bytes_accessed=2**12, transcendentals=0),
    )(me, cid, rank.reshape(1, rows))
    early = range(half, nodes)
    messages = [None] * nodes
    given = embeddings
    for chosen in (list(early), [g for g in range(nodes) if g not in early]):
        first = given is embeddings
        packed = pl.pallas_call(
            functools.partial(pack_kernel, chosen=chosen, capacity=capacity, first=first),
            out_shape=[jax.ShapeDtypeStruct((height, LANES), jnp.bfloat16)] * len(chosen)
            + [jax.ShapeDtypeStruct((rows, width + LANES), jnp.bfloat16)] * first,
            in_specs=[VMEM] * 3,
            out_specs=[VMEM] * (len(chosen) + first),
            compiler_params=PARAMS,
            cost_estimate=pl.CostEstimate(
                flops=2 * len(chosen) * capacity * rows * (width + LANES),
                bytes_accessed=2**12,
                transcendentals=0,
            ),
        )(given, target, digits)
        for g, message in zip(chosen, packed):
            messages[g] = message
        given = packed[-1]
    for g in range(1, nodes):
        messages[g] = lax.ppermute(messages[g], "ingest", [(i, i ^ flips[g]) for i in range(nodes)])

    def across(rows):
        return lax.ppermute(rows, "span", [(0, 1), (1, 0)])

    b, b_line = assemble(messages[half:], half, [], [], width)
    (best_b,) = match([(b, b_line)], [b], [(0, 0)], {}, width)
    a, a_line = assemble(messages[:half], half, [best_b], [], width)
    groups = [(a, a_line), (b, b_line)]
    b_other = across(b)
    best_a, for_other = match([(a, a_line)], [b_other], [(0, 0)], {}, width, {(0, 0): 1}, foreign=1)
    from_other = across(for_other)
    best_a, best_b = match(
        groups,
        [b, a, b_other],
        [(0, 1), (0, 0), (1, 2)],
        {0: best_a, 1: best_b},
        width,
        {(0, 0): 1},
    )
    (best_a,) = match([(a, a_line)], [across(a)], [(0, 0)], {0: best_a}, width)
    highest = pl.pallas_call(
        functools.partial(address_kernel, flips=flips, capacity=capacity),
        out_shape=jax.ShapeDtypeStruct((nodes, 1, LANES), jnp.float32),
        in_specs=[SMEM] + [VMEM] * 3,
        out_specs=VMEM,
        compiler_params=PARAMS,
    )(me, best_a, best_b, from_other)
    back = lax.all_to_all(
        highest,
        "ingest",
        split_axis=0,
        concat_axis=0,
        tiled=True,
        axis_index_groups=[list(range(nodes))[::-1]],
    )
    result = pl.pallas_call(
        unpack_kernel,
        out_shape=jax.ShapeDtypeStruct((1, rows), jnp.float32),
        in_specs=[VMEM] * 3,
        out_specs=VMEM,
        compiler_params=PARAMS,
    )(back, cid, pos)
    return result.reshape(rows)


def solution(mesh):
    in_specs = (P(("ingest", "span"), None), P(("ingest", "span")), P(("ingest", "span")))
    out_specs = P(("ingest", "span"))
    return jax.shard_map(body, mesh=mesh, in_specs=in_specs, out_specs=out_specs, check_vma=False)
```

```python
import functools

import jax
import jax.numpy as jnp
from jax import lax
from jax.experimental import pallas as pl
from jax.experimental.pallas import tpu as pltpu
from jax.sharding import PartitionSpec as P

LANES = 128
EXTRA = 16
NEVER = 2.0**24
TILE = 512
PIECE = 256
PARAMS = pltpu.CompilerParams(vmem_limit_bytes=40 * 2**20)
VMEM = pl.BlockSpec(memory_space=pltpu.VMEM)
SMEM = pl.BlockSpec(memory_space=pltpu.SMEM)
ANY = pl.BlockSpec(memory_space=pl.ANY)


LIGHT = pl.CostEstimate(flops=1, bytes_accessed=1, transcendentals=0)


def membership(cid, nodes, rows):
    return lax.broadcasted_iota(jnp.int32, (nodes, rows), 0) == cid


def partners(nodes):
    half = nodes // 2
    quarter = half // 2
    far = [flip for i in range(quarter) for flip in (half + quarter + i, half + i)]
    near = [*range(quarter, half), *range(1, quarter)]
    sequence = [far[0]]
    for pair in zip(near, far[1:]):
        sequence.extend(pair)
    flips = [0] * nodes
    for g, flip in zip([*range(half + 3, nodes), *range(half, half + 3), *range(1, half)], sequence):
        flips[g] = flip
    return flips


def place_kernel(me_ref, cid_ref, rank_ref, pos_ref, target_ref, digits_ref, *, flips, capacity):
    nodes = len(flips)
    rows = cid_ref.shape[1]
    flip = cid_ref[...] ^ me_ref[0]
    slot = jnp.zeros_like(flip)
    for g, value in enumerate(flips):
        slot = jnp.where(flip == value, g, slot)
    chunks = [slice(i, i + LANES) for i in range(0, rows, LANES)]
    members = [membership(slot[:, at], nodes, LANES) for at in chunks]
    ahead = lax.broadcasted_iota(jnp.int32, (LANES, LANES), 0) < lax.broadcasted_iota(
        jnp.int32, (LANES, LANES), 1
    )
    ones = [member.astype(jnp.float32) for member in members]
    within = jnp.dot(
        jnp.concatenate(ones, axis=0).astype(jnp.bfloat16),
        ahead.astype(jnp.float32).astype(jnp.bfloat16),
        preferred_element_type=jnp.float32,
    )
    before = jnp.zeros((nodes, 1), jnp.float32)
    for i, at in enumerate(chunks):
        counts = within[i * nodes : (i + 1) * nodes, :] + before
        pos = jnp.sum(jnp.where(members[i], counts, 0.0), axis=0, keepdims=True).astype(jnp.int32)
        pos_ref[:, at] = pos
        target_ref[:, at] = slot[:, at] * capacity + pos
        before = before + jnp.sum(ones[i], axis=1, keepdims=True)
        shown = rank_ref[:, at] + 1
        digit = lax.broadcasted_iota(jnp.int32, (LANES, LANES), 0)
        digits = jnp.where(
            digit == 0,
            shown & 127,
            jnp.where(digit == 1, (shown >> 7) & 127, jnp.where(digit == 2, (shown >> 14) & 127, 0)),
        ).astype(jnp.float32)
        digits_ref[at, :] = jnp.transpose(digits).astype(jnp.bfloat16)


def pack_kernel(rows_ref, target_ref, digits_ref, *refs, chosen, capacity, first):
    *out_refs, whole_ref = refs if first else (*refs, None)
    rows = rows_ref.shape[0]
    slot = lax.broadcasted_iota(jnp.int32, (capacity, rows), 0)
    place = [(slot + g * capacity == target_ref[...]).astype(jnp.float32) for g in chosen]
    place = jnp.concatenate(place, axis=0).astype(jnp.bfloat16)
    if first:
        widened = rows_ref[...].astype(jnp.float32)
        squares = jnp.sum(widened * widened, axis=1, keepdims=True)
        normed = (widened * lax.rsqrt(squares + 1e-06)).astype(jnp.bfloat16)
        whole = jnp.concatenate([normed, digits_ref[...]], axis=1)
        whole_ref[...] = whole
    else:
        whole = rows_ref[...]
    width = whole.shape[1] - LANES
    pieces = width // LANES
    moved = jnp.dot(place, whole, preferred_element_type=jnp.float32)
    for i, out_ref in enumerate(out_refs):
        at = slice(i * capacity, (i + 1) * capacity)
        for p in range(pieces):
            out_ref[p * capacity : (p + 1) * capacity, :] = moved[
                at, p * LANES : (p + 1) * LANES
            ].astype(jnp.bfloat16)
        square = jnp.concatenate(
            [moved[at, width:], jnp.zeros((LANES - capacity, LANES), jnp.float32)], axis=0
        )
        out_ref[pieces * capacity :, :] = jnp.transpose(square)[0:EXTRA, :].astype(jnp.bfloat16)


def assemble_kernel(*refs, messages, capacity, pieces):
    sources, (rows_ref, line_ref) = refs[:messages], refs[-2:]
    if len(sources[0].shape) == 3:
        sources = [sources[0].at[i] for i in range(sources[0].shape[0])]
    for i, source in enumerate(sources):
        for p in range(pieces):
            rows_ref[i * capacity : (i + 1) * capacity, p * LANES : (p + 1) * LANES] = source[
                p * capacity : (p + 1) * capacity, :
            ]
        tile = source[pieces * capacity :, :].astype(jnp.float32)
        square = jnp.concatenate([tile, jnp.zeros((LANES - EXTRA, LANES), jnp.float32)], axis=0)
        rows_ref[i * capacity : (i + 1) * capacity, pieces * LANES :] = jnp.transpose(square)[
            0:capacity, :
        ].astype(jnp.bfloat16)
        line = tile[0:1, :] + 128.0 * tile[1:2, :] + 16384.0 * tile[2:3, :]
        line_ref[0:1, i * capacity : (i + 1) * capacity] = line[:, 0:capacity]


def assemble(messages, count, after, held, width):
    pieces = width // LANES
    capacity = (messages[0].shape[-2] - EXTRA) // pieces
    rows = count * capacity
    ahead = len(messages) + len(after)
    return pl.pallas_call(
        functools.partial(assemble_kernel, messages=len(messages), capacity=capacity, pieces=pieces),
        out_shape=[jax.ShapeDtypeStruct(h.shape, h.dtype) for h in held]
        + [
            jax.ShapeDtypeStruct((rows, width + LANES), jnp.bfloat16),
            jax.ShapeDtypeStruct((8, rows), jnp.float32),
        ],
        in_specs=[VMEM] * len(messages) + [ANY] * (len(after) + len(held)),
        out_specs=[ANY] * len(held) + [VMEM, VMEM],
        input_output_aliases={ahead + i: i for i in range(len(held))},
        compiler_params=PARAMS,
        cost_estimate=LIGHT,
    )(*messages, *after, *held)


def match_kernel(*refs, width, queries, candidates, foreign, pairs, mirrored, carried):
    q_refs, refs = refs[:queries], refs[queries:]
    line_refs, refs = refs[:queries], refs[queries:]
    k_refs, refs = refs[:candidates], refs[candidates:]
    carry_refs, out_refs = dict(zip(carried, refs)), refs[len(carried) :]
    best = {}
    for q in range(queries + foreign):
        rows = out_refs[q].shape[1]
        start = carry_refs[q][0:1, :] if q in carry_refs else jnp.full((1, rows), -1.0, jnp.float32)
        best[q] = [start[:, first : first + PIECE] for first in range(0, rows, PIECE)]
    for k in range(candidates):
        for first in range(0, k_refs[k].shape[0], TILE):
            at = slice(first, min(first + TILE, k_refs[k].shape[0]))
            tile = k_refs[k][at, width:].astype(jnp.float32)
            theirs = tile[:, 0:1] + 128.0 * tile[:, 1:2] + 16384.0 * tile[:, 2:3]
            other = jnp.where(theirs > 0.0, theirs, NEVER)
            for q in range(queries):
                if (q, k) not in pairs:
                    continue
                folded = None
                for piece, low in enumerate(range(0, q_refs[q].shape[0], PIECE)):
                    part = slice(low, low + PIECE)
                    scores = lax.dot_general(
                        k_refs[k][at, 0:width],
                        q_refs[q][part, 0:width],
                        (((1,), (1,)), ((), ())),
                        preferred_element_type=jnp.float32,
                    )
                    line = line_refs[q][0:1, part]
                    kept = jnp.where(other < line, scores, -1.0)
                    found = jnp.max(kept, axis=0, keepdims=True)
                    best[q][piece] = jnp.maximum(best[q][piece], found)
                    if (q, k) in mirrored:
                        line = jnp.where(line > 0.0, line, NEVER)
                        kept = jnp.where(line < theirs, scores, -1.0)
                        for lane in range(0, PIECE, LANES):
                            column = kept[:, lane : lane + LANES]
                            folded = column if folded is None else jnp.maximum(folded, column)
                if (q, k) in mirrored:
                    found = jnp.max(jnp.transpose(folded), axis=0, keepdims=True)
                    asked = best[mirrored[q, k]]
                    for piece in range(len(asked)):
                        part = slice(piece * PIECE, (piece + 1) * PIECE)
                        asked[piece] = jnp.maximum(asked[piece], found[:, part])
    for q in range(queries + foreign):
        out_refs[q][0:1, :] = jnp.concatenate(best[q], axis=1)


def match(groups, candidates, pairs, carry, width, mirrored=None, foreign=0):
    carried = tuple(sorted(carry))
    operands = [
        *[rows for rows, _ in groups],
        *[line for _, line in groups],
        *candidates,
        *[carry[q] for q in carried],
    ]
    return pl.pallas_call(
        functools.partial(
            match_kernel,
            width=width,
            queries=len(groups),
            candidates=len(candidates),
            foreign=foreign,
            pairs=frozenset(pairs),
            mirrored=mirrored or {},
            carried=carried,
        ),
        out_shape=[jax.ShapeDtypeStruct(line.shape, jnp.float32) for _, line in groups]
        + [jax.ShapeDtypeStruct(groups[0][1].shape, jnp.float32)] * foreign,
        in_specs=[VMEM] * len(operands),
        out_specs=[VMEM] * (len(groups) + foreign),
        compiler_params=PARAMS,
        cost_estimate=LIGHT,
    )(*operands)


def address_kernel(me_ref, first_ref, second_ref, other_ref, out_ref, *, flips, capacity):
    out_ref[...] = jnp.zeros(out_ref.shape, jnp.float32)
    second = jnp.maximum(second_ref[0:1, :], other_ref[0:1, :])
    lines = [first_ref[0:1, :], second]
    blocks = [(line, i) for line in lines for i in range(line.shape[1] // capacity)]
    for flip, (line, i) in zip(flips, blocks):
        out_ref[(out_ref.shape[0] - 1) - (me_ref[0] ^ flip), 0:1, 0:capacity] = line[
            :, i * capacity : (i + 1) * capacity
        ]


def unpack_kernel(back_ref, cid_ref, pos_ref, out_ref):
    nodes = back_ref.shape[0]
    lines = jnp.concatenate([back_ref[g] for g in range(nodes)], axis=0)
    for first in range(0, cid_ref.shape[1], LANES):
        at = slice(first, first + LANES)
        index = jnp.broadcast_to(pos_ref[:, at], (nodes, LANES))
        found = jnp.take_along_axis(lines, index, axis=1, mode="promise_in_bounds")
        member = membership((nodes - 1) - cid_ref[:, at], nodes, LANES)
        out_ref[:, at] = jnp.sum(jnp.where(member, found, 0.0), axis=0, keepdims=True)


def body(embeddings, cluster_id, rank):
    nodes = lax.axis_size("ingest")
    rows, width = embeddings.shape
    capacity = 2 * rows // nodes
    height = capacity * (width // LANES) + EXTRA
    cid = cluster_id.reshape(1, rows)
    half = nodes // 2
    me = lax.axis_index("ingest").astype(jnp.int32).reshape(1)
    flips = partners(nodes)
    pos, target, digits = pl.pallas_call(
        functools.partial(place_kernel, flips=flips, capacity=capacity),
        out_shape=(
            jax.ShapeDtypeStruct((1, rows), jnp.int32),
            jax.ShapeDtypeStruct((1, rows), jnp.int32),
            jax.ShapeDtypeStruct((rows, LANES), jnp.bfloat16),
        ),
        in_specs=[SMEM] + [VMEM] * 2,
        out_specs=[VMEM] * 3,
        compiler_params=PARAMS,
        cost_estimate=pl.CostEstimate(flops=2**28, bytes_accessed=2**12, transcendentals=0),
    )(me, cid, rank.reshape(1, rows))
    early = range(half, nodes)
    messages = [None] * nodes
    given = embeddings
    for chosen in (list(early), [g for g in range(nodes) if g not in early]):
        first = given is embeddings
        packed = pl.pallas_call(
            functools.partial(pack_kernel, chosen=chosen, capacity=capacity, first=first),
            out_shape=[jax.ShapeDtypeStruct((height, LANES), jnp.bfloat16)] * len(chosen)
            + [jax.ShapeDtypeStruct((rows, width + LANES), jnp.bfloat16)] * first,
            in_specs=[VMEM] * 3,
            out_specs=[VMEM] * (len(chosen) + first),
            compiler_params=PARAMS,
            cost_estimate=pl.CostEstimate(
                flops=2 * len(chosen) * capacity * rows * (width + LANES),
                bytes_accessed=2**12,
                transcendentals=0,
            ),
        )(given, target, digits)
        for g, message in zip(chosen, packed):
            messages[g] = message
        given = packed[-1]
    for g in range(1, nodes):
        messages[g] = lax.ppermute(messages[g], "ingest", [(i, i ^ flips[g]) for i in range(nodes)])

    def across(rows):
        return lax.ppermute(rows, "span", [(0, 1), (1, 0)])

    b, b_line = assemble(messages[half:], half, [], [], width)
    (best_b,) = match([(b, b_line)], [b], [(0, 0)], {}, width)
    a, a_line = assemble(messages[:half], half, [best_b], [], width)
    groups = [(a, a_line), (b, b_line)]
    b_other = across(b)
    best_a, for_other = match([(a, a_line)], [b_other], [(0, 0)], {}, width, {(0, 0): 1}, foreign=1)
    from_other = across(for_other)
    best_a, best_b = match(
        groups,
        [b, a, b_other],
        [(0, 1), (0, 0), (1, 2)],
        {0: best_a, 1: best_b},
        width,
        {(0, 0): 1},
    )
    (best_a,) = match([(a, a_line)], [across(a)], [(0, 0)], {0: best_a}, width)
    highest = pl.pallas_call(
        functools.partial(address_kernel, flips=flips, capacity=capacity),
        out_shape=jax.ShapeDtypeStruct((nodes, 1, LANES), jnp.float32),
        in_specs=[SMEM] + [VMEM] * 3,
        out_specs=VMEM,
        compiler_params=PARAMS,
    )(me, best_a, best_b, from_other)
    back = lax.all_to_all(
        highest,
        "ingest",
        split_axis=0,
        concat_axis=0,
        tiled=True,
        axis_index_groups=[list(range(nodes))[::-1]],
    )
    result = pl.pallas_call(
        unpack_kernel,
        out_shape=jax.ShapeDtypeStruct((1, rows), jnp.float32),
        in_specs=[VMEM] * 3,
        out_specs=VMEM,
        compiler_params=PARAMS,
    )(back, cid, pos)
    return result.reshape(rows)


def solution(mesh):
    in_specs = (P(("ingest", "span"), None), P(("ingest", "span")), P(("ingest", "span")))
    out_specs = P(("ingest", "span"))
    return jax.shard_map(body, mesh=mesh, in_specs=in_specs, out_specs=out_specs, check_vma=False)
```

```python
import functools

import jax
import jax.numpy as jnp
from jax import lax
from jax.experimental import pallas as pl
from jax.experimental.pallas import tpu as pltpu
from jax.sharding import PartitionSpec as P

LANES = 128
EXTRA = 16
NEVER = 2.0**24
TILE = 512
PIECE = 256
PARAMS = pltpu.CompilerParams(vmem_limit_bytes=40 * 2**20)
VMEM = pl.BlockSpec(memory_space=pltpu.VMEM)
SMEM = pl.BlockSpec(memory_space=pltpu.SMEM)
ANY = pl.BlockSpec(memory_space=pl.ANY)


LIGHT = pl.CostEstimate(flops=1, bytes_accessed=1, transcendentals=0)


def membership(cid, nodes, rows):
    return lax.broadcasted_iota(jnp.int32, (nodes, rows), 0) == cid


def partners(nodes):
    half = nodes // 2
    quarter = half // 2
    far = [flip for i in range(quarter) for flip in (half + quarter + i, half + i)]
    near = [*range(quarter, half), *range(1, quarter)]
    sequence = [far[0]]
    for pair in zip(near, far[1:]):
        sequence.extend(pair)
    flips = [0] * nodes
    for g, flip in zip([*range(half + 3, nodes), *range(half, half + 3), *range(1, half)], sequence):
        flips[g] = flip
    return flips


def place_kernel(me_ref, cid_ref, rank_ref, pos_ref, target_ref, digits_ref, *, flips, capacity):
    nodes = len(flips)
    rows = cid_ref.shape[1]
    flip = cid_ref[...] ^ me_ref[0]
    slot = jnp.zeros_like(flip)
    for g, value in enumerate(flips):
        slot = jnp.where(flip == value, g, slot)
    chunks = [slice(i, i + LANES) for i in range(0, rows, LANES)]
    members = [membership(slot[:, at], nodes, LANES) for at in chunks]
    ahead = lax.broadcasted_iota(jnp.int32, (LANES, LANES), 0) < lax.broadcasted_iota(
        jnp.int32, (LANES, LANES), 1
    )
    ones = [member.astype(jnp.float32) for member in members]
    within = jnp.dot(
        jnp.concatenate(ones, axis=0).astype(jnp.bfloat16),
        ahead.astype(jnp.float32).astype(jnp.bfloat16),
        preferred_element_type=jnp.float32,
    )
    before = jnp.zeros((nodes, 1), jnp.float32)
    for i, at in enumerate(chunks):
        counts = within[i * nodes : (i + 1) * nodes, :] + before
        pos = jnp.sum(jnp.where(members[i], counts, 0.0), axis=0, keepdims=True).astype(jnp.int32)
        pos_ref[:, at] = pos
        target_ref[:, at] = slot[:, at] * capacity + pos
        before = before + jnp.sum(ones[i], axis=1, keepdims=True)
        shown = rank_ref[:, at] + 1
        digit = lax.broadcasted_iota(jnp.int32, (LANES, LANES), 0)
        digits = jnp.where(
            digit == 0,
            shown & 127,
            jnp.where(digit == 1, (shown >> 7) & 127, jnp.where(digit == 2, (shown >> 14) & 127, 0)),
        ).astype(jnp.float32)
        digits_ref[at, :] = jnp.transpose(digits).astype(jnp.bfloat16)


def pack_kernel(rows_ref, target_ref, digits_ref, *refs, chosen, capacity, first):
    *out_refs, whole_ref = refs if first else (*refs, None)
    rows = rows_ref.shape[0]
    slot = lax.broadcasted_iota(jnp.int32, (capacity, rows), 0)
    place = [(slot + g * capacity == target_ref[...]).astype(jnp.float32) for g in chosen]
    place = jnp.concatenate(place, axis=0).astype(jnp.bfloat16)
    if first:
        widened = rows_ref[...].astype(jnp.float32)
        squares = jnp.sum(widened * widened, axis=1, keepdims=True)
        normed = (widened * lax.rsqrt(squares + 1e-06)).astype(jnp.bfloat16)
        whole = jnp.concatenate([normed, digits_ref[...]], axis=1)
        whole_ref[...] = whole
    else:
        whole = rows_ref[...]
    width = whole.shape[1] - LANES
    pieces = width // LANES
    moved = jnp.dot(place, whole, preferred_element_type=jnp.float32)
    for i, out_ref in enumerate(out_refs):
        at = slice(i * capacity, (i + 1) * capacity)
        for p in range(pieces):
            out_ref[p * capacity : (p + 1) * capacity, :] = moved[
                at, p * LANES : (p + 1) * LANES
            ].astype(jnp.bfloat16)
        square = jnp.concatenate(
            [moved[at, width:], jnp.zeros((LANES - capacity, LANES), jnp.float32)], axis=0
        )
        out_ref[pieces * capacity :, :] = jnp.transpose(square)[0:EXTRA, :].astype(jnp.bfloat16)


def assemble_kernel(*refs, messages, capacity, pieces):
    sources, (rows_ref, line_ref) = refs[:messages], refs[-2:]
    if len(sources[0].shape) == 3:
        sources = [sources[0].at[i] for i in range(sources[0].shape[0])]
    for i, source in enumerate(sources):
        for p in range(pieces):
            rows_ref[i * capacity : (i + 1) * capacity, p * LANES : (p + 1) * LANES] = source[
                p * capacity : (p + 1) * capacity, :
            ]
        tile = source[pieces * capacity :, :].astype(jnp.float32)
        square = jnp.concatenate([tile, jnp.zeros((LANES - EXTRA, LANES), jnp.float32)], axis=0)
        rows_ref[i * capacity : (i + 1) * capacity, pieces * LANES :] = jnp.transpose(square)[
            0:capacity, :
        ].astype(jnp.bfloat16)
        line = tile[0:1, :] + 128.0 * tile[1:2, :] + 16384.0 * tile[2:3, :]
        line_ref[0:1, i * capacity : (i + 1) * capacity] = line[:, 0:capacity]


def assemble(messages, count, after, held, width):
    pieces = width // LANES
    capacity = (messages[0].shape[-2] - EXTRA) // pieces
    rows = count * capacity
    ahead = len(messages) + len(after)
    return pl.pallas_call(
        functools.partial(assemble_kernel, messages=len(messages), capacity=capacity, pieces=pieces),
        out_shape=[jax.ShapeDtypeStruct(h.shape, h.dtype) for h in held]
        + [
            jax.ShapeDtypeStruct((rows, width + LANES), jnp.bfloat16),
            jax.ShapeDtypeStruct((8, rows), jnp.float32),
        ],
        in_specs=[VMEM] * len(messages) + [ANY] * (len(after) + len(held)),
        out_specs=[ANY] * len(held) + [VMEM, VMEM],
        input_output_aliases={ahead + i: i for i in range(len(held))},
        compiler_params=PARAMS,
        cost_estimate=LIGHT,
    )(*messages, *after, *held)


def match_kernel(*refs, width, queries, candidates, foreign, pairs, mirrored, carried):
    q_refs, refs = refs[:queries], refs[queries:]
    line_refs, refs = refs[:queries], refs[queries:]
    k_refs, refs = refs[:candidates], refs[candidates:]
    carry_refs, out_refs = dict(zip(carried, refs)), refs[len(carried) :]
    best = {}
    for q in range(queries + foreign):
        rows = out_refs[q].shape[1]
        start = carry_refs[q][0:1, :] if q in carry_refs else jnp.full((1, rows), -1.0, jnp.float32)
        best[q] = [start[:, first : first + PIECE] for first in range(0, rows, PIECE)]
    for k in range(candidates):
        for first in range(0, k_refs[k].shape[0], TILE):
            at = slice(first, min(first + TILE, k_refs[k].shape[0]))
            tile = k_refs[k][at, width:].astype(jnp.float32)
            theirs = tile[:, 0:1] + 128.0 * tile[:, 1:2] + 16384.0 * tile[:, 2:3]
            other = jnp.where(theirs > 0.0, theirs, NEVER)
            for q in range(queries):
                if (q, k) not in pairs:
                    continue
                folded = None
                for piece, low in enumerate(range(0, q_refs[q].shape[0], PIECE)):
                    part = slice(low, low + PIECE)
                    scores = lax.dot_general(
                        k_refs[k][at, 0:width],
                        q_refs[q][part, 0:width],
                        (((1,), (1,)), ((), ())),
                        preferred_element_type=jnp.float32,
                    )
                    line = line_refs[q][0:1, part]
                    kept = jnp.where(other < line, scores, -1.0)
                    found = jnp.max(kept, axis=0, keepdims=True)
                    best[q][piece] = jnp.maximum(best[q][piece], found)
                    if (q, k) in mirrored:
                        line = jnp.where(line > 0.0, line, NEVER)
                        kept = jnp.where(line < theirs, scores, -1.0)
                        for lane in range(0, PIECE, LANES):
                            column = kept[:, lane : lane + LANES]
                            folded = column if folded is None else jnp.maximum(folded, column)
                if (q, k) in mirrored:
                    found = jnp.max(jnp.transpose(folded), axis=0, keepdims=True)
                    asked = best[mirrored[q, k]]
                    for piece in range(len(asked)):
                        part = slice(piece * PIECE, (piece + 1) * PIECE)
                        asked[piece] = jnp.maximum(asked[piece], found[:, part])
    for q in range(queries + foreign):
        out_refs[q][0:1, :] = jnp.concatenate(best[q], axis=1)


def match(groups, candidates, pairs, carry, width, mirrored=None, foreign=0):
    carried = tuple(sorted(carry))
    operands = [
        *[rows for rows, _ in groups],
        *[line for _, line in groups],
        *candidates,
        *[carry[q] for q in carried],
    ]
    return pl.pallas_call(
        functools.partial(
            match_kernel,
            width=width,
            queries=len(groups),
            candidates=len(candidates),
            foreign=foreign,
            pairs=frozenset(pairs),
            mirrored=mirrored or {},
            carried=carried,
        ),
        out_shape=[jax.ShapeDtypeStruct(line.shape, jnp.float32) for _, line in groups]
        + [jax.ShapeDtypeStruct(groups[0][1].shape, jnp.float32)] * foreign,
        in_specs=[VMEM] * len(operands),
        out_specs=[VMEM] * (len(groups) + foreign),
        compiler_params=PARAMS,
        cost_estimate=LIGHT,
    )(*operands)


def address_kernel(me_ref, first_ref, second_ref, other_ref, out_ref, *, flips, capacity):
    out_ref[...] = jnp.zeros(out_ref.shape, jnp.float32)
    second = jnp.maximum(second_ref[0:1, :], other_ref[0:1, :])
    lines = [first_ref[0:1, :], second]
    blocks = [(line, i) for line in lines for i in range(line.shape[1] // capacity)]
    for flip, (line, i) in zip(flips, blocks):
        out_ref[(out_ref.shape[0] - 1) - (me_ref[0] ^ flip), 0:1, 0:capacity] = line[
            :, i * capacity : (i + 1) * capacity
        ]


def unpack_kernel(back_ref, cid_ref, pos_ref, out_ref):
    nodes = back_ref.shape[0]
    lines = jnp.concatenate([back_ref[g] for g in range(nodes)], axis=0)
    for first in range(0, cid_ref.shape[1], LANES):
        at = slice(first, first + LANES)
        index = jnp.broadcast_to(pos_ref[:, at], (nodes, LANES))
        found = jnp.take_along_axis(lines, index, axis=1, mode="promise_in_bounds")
        member = membership((nodes - 1) - cid_ref[:, at], nodes, LANES)
        out_ref[:, at] = jnp.sum(jnp.where(member, found, 0.0), axis=0, keepdims=True)


def body(embeddings, cluster_id, rank):
    nodes = lax.axis_size("ingest")
    rows, width = embeddings.shape
    capacity = 2 * rows // nodes
    height = capacity * (width // LANES) + EXTRA
    cid = cluster_id.reshape(1, rows)
    half = nodes // 2
    me = lax.axis_index("ingest").astype(jnp.int32).reshape(1)
    flips = partners(nodes)
    pos, target, digits = pl.pallas_call(
        functools.partial(place_kernel, flips=flips, capacity=capacity),
        out_shape=(
            jax.ShapeDtypeStruct((1, rows), jnp.int32),
            jax.ShapeDtypeStruct((1, rows), jnp.int32),
            jax.ShapeDtypeStruct((rows, LANES), jnp.bfloat16),
        ),
        in_specs=[SMEM] + [VMEM] * 2,
        out_specs=[VMEM] * 3,
        compiler_params=PARAMS,
        cost_estimate=pl.CostEstimate(flops=2**28, bytes_accessed=2**12, transcendentals=0),
    )(me, cid, rank.reshape(1, rows))
    early = range(half, nodes)
    messages = [None] * nodes
    given = embeddings
    for chosen in (list(early), [g for g in range(nodes) if g not in early]):
        first = given is embeddings
        packed = pl.pallas_call(
            functools.partial(pack_kernel, chosen=chosen, capacity=capacity, first=first),
            out_shape=[jax.ShapeDtypeStruct((height, LANES), jnp.bfloat16)] * len(chosen)
            + [jax.ShapeDtypeStruct((rows, width + LANES), jnp.bfloat16)] * first,
            in_specs=[VMEM] * 3,
            out_specs=[VMEM] * (len(chosen) + first),
            compiler_params=PARAMS,
            cost_estimate=pl.CostEstimate(
                flops=2 * len(chosen) * capacity * rows * (width + LANES),
                bytes_accessed=2**12,
                transcendentals=0,
            ),
        )(given, target, digits)
        for g, message in zip(chosen, packed):
            messages[g] = message
        given = packed[-1]
    for g in range(1, nodes):
        messages[g] = lax.ppermute(messages[g], "ingest", [(i, i ^ flips[g]) for i in range(nodes)])

    def across(rows):
        return lax.ppermute(rows, "span", [(0, 1), (1, 0)])

    b, b_line = assemble(messages[half:], half, [], [], width)
    (best_b,) = match([(b, b_line)], [b], [(0, 0)], {}, width)
    a, a_line = assemble(messages[:half], half, [best_b], [], width)
    groups = [(a, a_line), (b, b_line)]
    best_a, best_b, for_other = match(
        groups,
        [across(b), b, a],
        [(0, 0), (1, 0), (0, 1), (0, 2)],
        {1: best_b},
        width,
        {(0, 0): 2, (0, 1): 1},
        foreign=1,
    )
    from_other = across(for_other)
    (best_a,) = match([(a, a_line)], [across(a)], [(0, 0)], {0: best_a}, width)
    highest = pl.pallas_call(
        functools.partial(address_kernel, flips=flips, capacity=capacity),
        out_shape=jax.ShapeDtypeStruct((nodes, 1, LANES), jnp.float32),
        in_specs=[SMEM] + [VMEM] * 3,
        out_specs=VMEM,
        compiler_params=PARAMS,
    )(me, best_a, best_b, from_other)
    back = lax.all_to_all(
        highest,
        "ingest",
        split_axis=0,
        concat_axis=0,
        tiled=True,
        axis_index_groups=[list(range(nodes))[::-1]],
    )
    result = pl.pallas_call(
        unpack_kernel,
        out_shape=jax.ShapeDtypeStruct((1, rows), jnp.float32),
        in_specs=[VMEM] * 3,
        out_specs=VMEM,
        compiler_params=PARAMS,
    )(back, cid, pos)
    return result.reshape(rows)


def solution(mesh):
    in_specs = (P(("ingest", "span"), None), P(("ingest", "span")), P(("ingest", "span")))
    out_specs = P(("ingest", "span"))
    return jax.shard_map(body, mesh=mesh, in_specs=in_specs, out_specs=out_specs, check_vma=False)
```

```python
import functools

import jax
import jax.numpy as jnp
from jax import lax
from jax.experimental import pallas as pl
from jax.experimental.pallas import tpu as pltpu
from jax.sharding import PartitionSpec as P

LANES = 128
EXTRA = 16
NEVER = 2.0**24
TILE = 512
PIECE = 256
PARAMS = pltpu.CompilerParams(vmem_limit_bytes=40 * 2**20)
VMEM = pl.BlockSpec(memory_space=pltpu.VMEM)
SMEM = pl.BlockSpec(memory_space=pltpu.SMEM)
ANY = pl.BlockSpec(memory_space=pl.ANY)


LIGHT = pl.CostEstimate(flops=1, bytes_accessed=1, transcendentals=0)


def membership(cid, nodes, rows):
    return lax.broadcasted_iota(jnp.int32, (nodes, rows), 0) == cid


def partners(nodes):
    half = nodes // 2
    far = [half, nodes - 1, *range(half + half // 2, nodes - 1), *range(half + 1, half + half // 2)]
    near = [1, *range(half // 2, half), *range(2, half // 2)]
    sequence = [far[0]]
    for pair in zip(near, far[1:]):
        sequence.extend(pair)
    flips = [0] * nodes
    for g, flip in zip([*range(half + 3, nodes), *range(half, half + 3), *range(1, half)], sequence):
        flips[g] = flip
    return flips


def place_kernel(me_ref, cid_ref, rank_ref, pos_ref, target_ref, digits_ref, *, flips, capacity):
    nodes = len(flips)
    rows = cid_ref.shape[1]
    flip = cid_ref[...] ^ me_ref[0]
    slot = jnp.zeros_like(flip)
    for g, value in enumerate(flips):
        slot = jnp.where(flip == value, g, slot)
    chunks = [slice(i, i + LANES) for i in range(0, rows, LANES)]
    members = [membership(slot[:, at], nodes, LANES) for at in chunks]
    ahead = lax.broadcasted_iota(jnp.int32, (LANES, LANES), 0) < lax.broadcasted_iota(
        jnp.int32, (LANES, LANES), 1
    )
    ones = [member.astype(jnp.float32) for member in members]
    within = jnp.dot(
        jnp.concatenate(ones, axis=0).astype(jnp.bfloat16),
        ahead.astype(jnp.float32).astype(jnp.bfloat16),
        preferred_element_type=jnp.float32,
    )
    before = jnp.zeros((nodes, 1), jnp.float32)
    for i, at in enumerate(chunks):
        counts = within[i * nodes : (i + 1) * nodes, :] + before
        pos = jnp.sum(jnp.where(members[i], counts, 0.0), axis=0, keepdims=True).astype(jnp.int32)
        pos_ref[:, at] = pos
        target_ref[:, at] = slot[:, at] * capacity + pos
        before = before + jnp.sum(ones[i], axis=1, keepdims=True)
        shown = rank_ref[:, at] + 1
        digit = lax.broadcasted_iota(jnp.int32, (LANES, LANES), 0)
        digits = jnp.where(
            digit == 0,
            shown & 127,
            jnp.where(digit == 1, (shown >> 7) & 127, jnp.where(digit == 2, (shown >> 14) & 127, 0)),
        ).astype(jnp.float32)
        digits_ref[at, :] = jnp.transpose(digits).astype(jnp.bfloat16)


def pack_kernel(rows_ref, target_ref, digits_ref, *refs, chosen, capacity, first):
    *out_refs, whole_ref = refs if first else (*refs, None)
    rows = rows_ref.shape[0]
    slot = lax.broadcasted_iota(jnp.int32, (capacity, rows), 0)
    place = [(slot + g * capacity == target_ref[...]).astype(jnp.float32) for g in chosen]
    place = jnp.concatenate(place, axis=0).astype(jnp.bfloat16)
    if first:
        widened = rows_ref[...].astype(jnp.float32)
        squares = jnp.sum(widened * widened, axis=1, keepdims=True)
        normed = (widened * lax.rsqrt(squares + 1e-06)).astype(jnp.bfloat16)
        whole = jnp.concatenate([normed, digits_ref[...]], axis=1)
        whole_ref[...] = whole
    else:
        whole = rows_ref[...]
    width = whole.shape[1] - LANES
    pieces = width // LANES
    moved = jnp.dot(place, whole, preferred_element_type=jnp.float32)
    for i, out_ref in enumerate(out_refs):
        at = slice(i * capacity, (i + 1) * capacity)
        for p in range(pieces):
            out_ref[p * capacity : (p + 1) * capacity, :] = moved[
                at, p * LANES : (p + 1) * LANES
            ].astype(jnp.bfloat16)
        square = jnp.concatenate(
            [moved[at, width:], jnp.zeros((LANES - capacity, LANES), jnp.float32)], axis=0
        )
        out_ref[pieces * capacity :, :] = jnp.transpose(square)[0:EXTRA, :].astype(jnp.bfloat16)


def assemble_kernel(*refs, messages, capacity, pieces):
    sources, (rows_ref, line_ref) = refs[:messages], refs[-2:]
    if len(sources[0].shape) == 3:
        sources = [sources[0].at[i] for i in range(sources[0].shape[0])]
    for i, source in enumerate(sources):
        for p in range(pieces):
            rows_ref[i * capacity : (i + 1) * capacity, p * LANES : (p + 1) * LANES] = source[
                p * capacity : (p + 1) * capacity, :
            ]
        tile = source[pieces * capacity :, :].astype(jnp.float32)
        square = jnp.concatenate([tile, jnp.zeros((LANES - EXTRA, LANES), jnp.float32)], axis=0)
        rows_ref[i * capacity : (i + 1) * capacity, pieces * LANES :] = jnp.transpose(square)[
            0:capacity, :
        ].astype(jnp.bfloat16)
        line = tile[0:1, :] + 128.0 * tile[1:2, :] + 16384.0 * tile[2:3, :]
        line_ref[0:1, i * capacity : (i + 1) * capacity] = line[:, 0:capacity]


def assemble(messages, count, after, held, width):
    pieces = width // LANES
    capacity = (messages[0].shape[-2] - EXTRA) // pieces
    rows = count * capacity
    ahead = len(messages) + len(after)
    return pl.pallas_call(
        functools.partial(assemble_kernel, messages=len(messages), capacity=capacity, pieces=pieces),
        out_shape=[jax.ShapeDtypeStruct(h.shape, h.dtype) for h in held]
        + [
            jax.ShapeDtypeStruct((rows, width + LANES), jnp.bfloat16),
            jax.ShapeDtypeStruct((8, rows), jnp.float32),
        ],
        in_specs=[VMEM] * len(messages) + [ANY] * (len(after) + len(held)),
        out_specs=[ANY] * len(held) + [VMEM, VMEM],
        input_output_aliases={ahead + i: i for i in range(len(held))},
        compiler_params=PARAMS,
        cost_estimate=LIGHT,
    )(*messages, *after, *held)


def match_kernel(*refs, width, queries, candidates, foreign, pairs, mirrored, carried):
    q_refs, refs = refs[:queries], refs[queries:]
    line_refs, refs = refs[:queries], refs[queries:]
    k_refs, refs = refs[:candidates], refs[candidates:]
    carry_refs, out_refs = dict(zip(carried, refs)), refs[len(carried) :]
    best = {}
    for q in range(queries + foreign):
        rows = out_refs[q].shape[1]
        start = carry_refs[q][0:1, :] if q in carry_refs else jnp.full((1, rows), -1.0, jnp.float32)
        best[q] = [start[:, first : first + PIECE] for first in range(0, rows, PIECE)]
    for k in range(candidates):
        for first in range(0, k_refs[k].shape[0], TILE):
            at = slice(first, min(first + TILE, k_refs[k].shape[0]))
            tile = k_refs[k][at, width:].astype(jnp.float32)
            theirs = tile[:, 0:1] + 128.0 * tile[:, 1:2] + 16384.0 * tile[:, 2:3]
            other = jnp.where(theirs > 0.0, theirs, NEVER)
            for q in range(queries):
                if (q, k) not in pairs:
                    continue
                folded = None
                for piece, low in enumerate(range(0, q_refs[q].shape[0], PIECE)):
                    part = slice(low, low + PIECE)
                    scores = lax.dot_general(
                        k_refs[k][at, 0:width],
                        q_refs[q][part, 0:width],
                        (((1,), (1,)), ((), ())),
                        preferred_element_type=jnp.float32,
                    )
                    line = line_refs[q][0:1, part]
                    kept = jnp.where(other < line, scores, -1.0)
                    found = jnp.max(kept, axis=0, keepdims=True)
                    best[q][piece] = jnp.maximum(best[q][piece], found)
                    if (q, k) in mirrored:
                        line = jnp.where(line > 0.0, line, NEVER)
                        kept = jnp.where(line < theirs, scores, -1.0)
                        for lane in range(0, PIECE, LANES):
                            column = kept[:, lane : lane + LANES]
                            folded = column if folded is None else jnp.maximum(folded, column)
                if (q, k) in mirrored:
                    found = jnp.max(jnp.transpose(folded), axis=0, keepdims=True)
                    asked = best[mirrored[q, k]]
                    for piece in range(len(asked)):
                        part = slice(piece * PIECE, (piece + 1) * PIECE)
                        asked[piece] = jnp.maximum(asked[piece], found[:, part])
    for q in range(queries + foreign):
        out_refs[q][0:1, :] = jnp.concatenate(best[q], axis=1)


def match(groups, candidates, pairs, carry, width, mirrored=None, foreign=0):
    carried = tuple(sorted(carry))
    operands = [
        *[rows for rows, _ in groups],
        *[line for _, line in groups],
        *candidates,
        *[carry[q] for q in carried],
    ]
    return pl.pallas_call(
        functools.partial(
            match_kernel,
            width=width,
            queries=len(groups),
            candidates=len(candidates),
            foreign=foreign,
            pairs=frozenset(pairs),
            mirrored=mirrored or {},
            carried=carried,
        ),
        out_shape=[jax.ShapeDtypeStruct(line.shape, jnp.float32) for _, line in groups]
        + [jax.ShapeDtypeStruct(groups[0][1].shape, jnp.float32)] * foreign,
        in_specs=[VMEM] * len(operands),
        out_specs=[VMEM] * (len(groups) + foreign),
        compiler_params=PARAMS,
        cost_estimate=LIGHT,
    )(*operands)


def address_kernel(me_ref, first_ref, second_ref, other_ref, out_ref, *, flips, capacity):
    out_ref[...] = jnp.zeros(out_ref.shape, jnp.float32)
    second = jnp.maximum(second_ref[0:1, :], other_ref[0:1, :])
    lines = [first_ref[0:1, :], second]
    blocks = [(line, i) for line in lines for i in range(line.shape[1] // capacity)]
    for flip, (line, i) in zip(flips, blocks):
        out_ref[(out_ref.shape[0] - 1) - (me_ref[0] ^ flip), 0:1, 0:capacity] = line[
            :, i * capacity : (i + 1) * capacity
        ]


def unpack_kernel(back_ref, cid_ref, pos_ref, out_ref):
    nodes = back_ref.shape[0]
    lines = jnp.concatenate([back_ref[g] for g in range(nodes)], axis=0)
    for first in range(0, cid_ref.shape[1], LANES):
        at = slice(first, first + LANES)
        index = jnp.broadcast_to(pos_ref[:, at], (nodes, LANES))
        found = jnp.take_along_axis(lines, index, axis=1, mode="promise_in_bounds")
        member = membership((nodes - 1) - cid_ref[:, at], nodes, LANES)
        out_ref[:, at] = jnp.sum(jnp.where(member, found, 0.0), axis=0, keepdims=True)


def body(embeddings, cluster_id, rank):
    nodes = lax.axis_size("ingest")
    rows, width = embeddings.shape
    capacity = 2 * rows // nodes
    height = capacity * (width // LANES) + EXTRA
    cid = cluster_id.reshape(1, rows)
    half = nodes // 2
    me = lax.axis_index("ingest").astype(jnp.int32).reshape(1)
    flips = partners(nodes)
    pos, target, digits = pl.pallas_call(
        functools.partial(place_kernel, flips=flips, capacity=capacity),
        out_shape=(
            jax.ShapeDtypeStruct((1, rows), jnp.int32),
            jax.ShapeDtypeStruct((1, rows), jnp.int32),
            jax.ShapeDtypeStruct((rows, LANES), jnp.bfloat16),
        ),
        in_specs=[SMEM] + [VMEM] * 2,
        out_specs=[VMEM] * 3,
        compiler_params=PARAMS,
        cost_estimate=pl.CostEstimate(flops=2**28, bytes_accessed=2**12, transcendentals=0),
    )(me, cid, rank.reshape(1, rows))
    early = range(half, nodes)
    messages = [None] * nodes
    given = embeddings
    for chosen in (list(early), [g for g in range(nodes) if g not in early]):
        first = given is embeddings
        packed = pl.pallas_call(
            functools.partial(pack_kernel, chosen=chosen, capacity=capacity, first=first),
            out_shape=[jax.ShapeDtypeStruct((height, LANES), jnp.bfloat16)] * len(chosen)
            + [jax.ShapeDtypeStruct((rows, width + LANES), jnp.bfloat16)] * first,
            in_specs=[VMEM] * 3,
            out_specs=[VMEM] * (len(chosen) + first),
            compiler_params=PARAMS,
            cost_estimate=pl.CostEstimate(
                flops=2 * len(chosen) * capacity * rows * (width + LANES),
                bytes_accessed=2**12,
                transcendentals=0,
            ),
        )(given, target, digits)
        for g, message in zip(chosen, packed):
            messages[g] = message
        given = packed[-1]
    for g in range(1, nodes):
        messages[g] = lax.ppermute(messages[g], "ingest", [(i, i ^ flips[g]) for i in range(nodes)])

    def across(rows):
        return lax.ppermute(rows, "span", [(0, 1), (1, 0)])

    b, b_line = assemble(messages[half:], half, [], [], width)
    (best_b,) = match([(b, b_line)], [b], [(0, 0)], {}, width)
    a, a_line = assemble(messages[:half], half, [best_b], [], width)
    groups = [(a, a_line), (b, b_line)]
    b_other = across(b)
    best_a, for_other = match([(a, a_line)], [b_other], [(0, 0)], {}, width, {(0, 0): 1}, foreign=1)
    from_other = across(for_other)
    best_a, best_b = match(
        groups,
        [b, a, b_other],
        [(0, 1), (0, 0), (1, 2)],
        {0: best_a, 1: best_b},
        width,
        {(0, 0): 1},
    )
    (best_a,) = match([(a, a_line)], [across(a)], [(0, 0)], {0: best_a}, width)
    highest = pl.pallas_call(
        functools.partial(address_kernel, flips=flips, capacity=capacity),
        out_shape=jax.ShapeDtypeStruct((nodes, 1, LANES), jnp.float32),
        in_specs=[SMEM] + [VMEM] * 3,
        out_specs=VMEM,
        compiler_params=PARAMS,
    )(me, best_a, best_b, from_other)
    back = lax.all_to_all(
        highest,
        "ingest",
        split_axis=0,
        concat_axis=0,
        tiled=True,
        axis_index_groups=[list(range(nodes))[::-1]],
    )
    result = pl.pallas_call(
        unpack_kernel,
        out_shape=jax.ShapeDtypeStruct((1, rows), jnp.float32),
        in_specs=[VMEM] * 3,
        out_specs=VMEM,
        compiler_params=PARAMS,
    )(back, cid, pos)
    return result.reshape(rows)


def solution(mesh):
    in_specs = (P(("ingest", "span"), None), P(("ingest", "span")), P(("ingest", "span")))
    out_specs = P(("ingest", "span"))
    return jax.shard_map(body, mesh=mesh, in_specs=in_specs, out_specs=out_specs, check_vma=False)
```
